256 devices in a mesh: col: 32 (over y, z), grp: 8 (over x, core).
Axes of the slice: x: 4, y: 4, z: 8, core: 2. Of those that a mesh axis runs over, the one named last changes fastest.
Arguments:
- velocity_cotangent: float32 [20, 8388608], P(None, ('col', 'grp')), may hold values from -6 to 6
- vertical_inverse: float32 [20, 20], replicated, may hold values from -1.25 to 1.25
- sliding_speed: float32 [8388608], P(('col', 'grp')), may hold values from 0.3 to 3
- friction_coef: float32 [8388608], P(('col', 'grp')), may hold values from 0.3 to 3
- thawed_bed: int32 [8388608], P(('col', 'grp')), may hold values 0 or 1
- basal_melt: float32 [8388608], P(('col', 'grp')), may hold values from 0 to 1
- storage_coef: float32 [8388608], P(('col', 'grp')), may hold values from 0.1 to 3
- owner_tile: int32 [8388608, 1], P(('col', 'grp')), may hold values from 0 to 31, as said below
- channel_open: int32 [256, 40960], P('grp', 'col'), may hold values 0 or 1
- group_mix: float32 [8, 8], replicated, may hold values from -2 to 2
- control_map: bfloat16 [16384, 32768], P(('col', 'grp')), may hold values from -0.03125 to 0.03125
Outputs:
- velocity_adjoint: float32 [20, 8388608], P(None, ('col', 'grp'))
- pressure_adjoint: float32 [256, 40960], P('grp', 'col')
- friction_sensitivity: float32 [8388608], P(('col', 'grp'))
- friction_gradient: float32 [16384], P(('col', 'grp'))
The draws below stay inside these ranges and needn't reach their ends.
Inputs may be any that keep to these rules, and one draw needn't show every extreme that they name: `owner_tile`: within each device's block of 32768 columns the tile indices never fall, no tile index appears more than 1280 times, and some tile index appears exactly 1280 times.
All inputs are finite; a program needn't handle non-finite values. No bound on the sum of `thawed_bed` or of `channel_open` on one device may be relied on, other than what follows from the above.
Results may differ from the reference program's by a relative error of at most 0.0027.
The reference program's roundings to bfloat16 on the way (of `mixed`) count: a program that leaves them out, or rounds other values in their place, can miss the bound.
Values sent between devices are 32-bit elements; how exact they have to be, the bound alone decides.
A program may use at most 64 MiB of HBM per device.

```python
import math
import jax
import jax.numpy as jnp
from jax import lax

LAYERS = 20
COLS_DEV = 32768
K_DEV = 64
HSWEEPS = 4
CAP = 1280
NCOLS = 8388608
HROWS = 256
HCOLS = 40960
NCTRL = 16384
N_COL = 32
N_GRP = 8


def draw_owner_tile(key, part):
    key = jax.random.fold_in(key, 7)
    block_count = N_COL * N_GRP
    remaining = COLS_DEV - CAP
    other_tiles = N_COL - 1
    even_share = remaining // other_tiles
    leftover = remaining % other_tiles
    wobble = min(even_share, CAP - even_share - 2)
    pair_count = other_tiles // 2
    block_keys = jax.random.split(key, block_count)

    def one_block(block_key):
        key_full, key_rank, key_size = jax.random.split(block_key, 3)
        full_tile = jax.random.randint(key_full, (), 0, N_COL)
        rank_of = jax.random.permutation(key_rank, other_tiles).astype(jnp.int32)
        amounts = jax.random.randint(key_size, (pair_count + 1,), 0, wobble + 1)
        pair_of = rank_of // 2
        in_pair = rank_of < 2 * pair_count
        signed = jnp.where(rank_of % 2 == 0, amounts[pair_of], -amounts[pair_of])
        change = jnp.where(in_pair, signed, 0) + (rank_of < leftover).astype(jnp.int32)
        other_counts = even_share + change
        tile_ids = jnp.arange(N_COL, dtype=jnp.int32)
        source_index = jnp.clip(tile_ids - (tile_ids > full_tile).astype(jnp.int32), 0, other_tiles - 1)
        counts = jnp.where(tile_ids == full_tile, CAP, other_counts[source_index])
        run_ends = jnp.cumsum(counts)
        column_ids = jnp.arange(COLS_DEV, dtype=jnp.int32)
        return jnp.sum((column_ids[:, None] >= run_ends[None, :]).astype(jnp.int32), axis=1)
    owners = lax.map(one_block, block_keys)
    return owners.reshape(-1, 1).astype(jnp.int32)


def with_ends(drawn, key, low, high):
    longest = drawn.shape.index(max(drawn.shape))
    spots = []
    for shift in (0, 1):
        where = [jax.random.randint(jax.random.fold_in(key, axis), (), 0, length) for axis, length in enumerate(drawn.shape)]
        where[longest] = (where[longest] + shift) % drawn.shape[longest]
        spots.append(tuple(where))
    return drawn.at[spots[0]].set(low).at[spots[1]].set(high)


def block_scale(rng, extent, pieces, smallest, high):
    level, own = 1.0, jax.random.fold_in(rng, 6)
    for dim, parts in pieces:
        heights = jnp.exp(jax.random.uniform(jax.random.fold_in(own, dim), (parts,), jnp.float32, smallest / len(pieces), high / len(pieces)))
        level = level * jnp.repeat(heights, extent[dim] // parts).reshape([-1 if axis == dim else 1 for axis in range(len(extent))])
    return level


def centred(own_key, extent, scale, limit, cuts=(), kind=jnp.bfloat16):
    entries = jax.random.normal(own_key, extent, jnp.float32) * scale
    if len(cuts) > 0:
        entries = block_scale(own_key, extent, cuts, -0.22, 0.18) * entries
    return jnp.clip(entries, min=-limit, max=limit).astype(kind)


def setup_inputs(seed: int = 0) -> dict:
    keys = jax.random.split(jax.random.key(seed), 12)
    return {
        "velocity_cotangent": centred(keys[0], (LAYERS, NCOLS), 1.0, 6.0, ((1, 256),), jnp.float32),
        "vertical_inverse": centred(keys[1], (LAYERS, LAYERS), LAYERS ** -0.5, 1.25, (), jnp.float32),
        "sliding_speed": jnp.clip(jnp.exp(math.log(3.0) - 2.3025851 * jax.random.uniform(keys[2], (NCOLS,), jnp.float32) ** block_scale(keys[2], (NCOLS,), ((0, 256),), -0.2, 0.2)), 0.3, 3.0),
        "friction_coef": jnp.clip(jnp.exp(math.log(3.0) - 2.3025851 * jax.random.uniform(keys[3], (NCOLS,), jnp.float32) ** block_scale(keys[3], (NCOLS,), ((0, 256),), -0.2, 0.2)), 0.3, 3.0),
        "thawed_bed": with_ends((jax.random.randint(keys[4], (NCOLS,), 0, 4) < 3).astype(jnp.int32), jax.random.fold_in(keys[4], 1), 0, 1),
        "basal_melt": jnp.clip(1.0 * jax.random.uniform(keys[5], (NCOLS,), jnp.float32) ** block_scale(keys[5], (NCOLS,), ((0, 256),), -0.2, 0.2), 0.0, 1.0),
        "storage_coef": jnp.clip(jnp.exp(math.log(3.0) - 3.4011974 * jax.random.uniform(keys[6], (NCOLS,), jnp.float32) ** block_scale(keys[6], (NCOLS,), ((0, 256),), -0.2, 0.2)), 0.1, 3.0),
        "owner_tile": draw_owner_tile(jax.random.fold_in(keys[11], 71), 0),
        "channel_open": with_ends((jax.random.randint(keys[8], (HROWS, HCOLS), 0, 4) < 1).astype(jnp.int32), jax.random.fold_in(keys[8], 1), 0, 1),
        "group_mix": centred(keys[9], (N_GRP, N_GRP), N_GRP ** -0.5, 2.0, (), jnp.float32),
        "control_map": centred(keys[10], (NCTRL, COLS_DEV), COLS_DEV ** -0.5, 0.03125, ((0, 256),)),
    }


diffusion_rate = 0.12
melt_rate = 0.3


def block_slots(targets):
    onehot = (targets[:, None] == jnp.arange(N_COL, dtype=jnp.int32)[None, :]).astype(jnp.int32)
    running = jnp.cumsum(onehot, axis=0)
    return (jnp.sum(running * onehot, axis=1) - 1).astype(jnp.int32)


def reference(velocity_cotangent, vertical_inverse, sliding_speed, friction_coef, thawed_bed, basal_melt, storage_coef, owner_tile, channel_open, group_mix, control_map):
    adjoint = jnp.dot(vertical_inverse.T, velocity_cotangent, precision=lax.Precision.HIGHEST, preferred_element_type=jnp.float32)
    thawed = thawed_bed.astype(jnp.float32)
    basal = thawed * sliding_speed * adjoint[LAYERS - 1]
    source = friction_coef * basal
    targets = owner_tile[:, 0].astype(jnp.int32)
    blocks = N_COL * N_GRP
    slots = lax.map(block_slots, targets.reshape(blocks, COLS_DEV)).reshape(-1)
    block_id = jnp.arange(NCOLS, dtype=jnp.int32) // COLS_DEV
    row_of = (block_id % N_GRP) * N_COL + block_id // N_GRP
    col_of = targets * CAP + slots
    values = jnp.stack([source, basal_melt, storage_coef])
    fields = jnp.zeros((3, HROWS, HCOLS), jnp.float32).at[:, row_of, col_of].set(values)
    conduct = jnp.where(channel_open == 1, 1.0, 0.25).astype(jnp.float32)
    coef = diffusion_rate * conduct / (1.0 + fields[2])
    keep = 1.0 - melt_rate * fields[1]
    pressure = fields[0]
    for sweep in range(HSWEEPS):
        padded = jnp.pad(pressure, 1)
        beside_all = padded[2:, 1:-1] + padded[:-2, 1:-1] + padded[1:-1, 2:] + padded[1:-1, :-2]
        pressure = keep * pressure + coef * (beside_all - 4.0 * pressure)
    back = pressure[row_of, col_of]
    sensitivity = thawed * friction_coef * (basal + back)
    grouped = sensitivity.reshape(N_COL, N_GRP, COLS_DEV)
    mixed = jnp.einsum("ij,ajc->aic", group_mix, grouped, precision=lax.Precision.HIGHEST).astype(jnp.bfloat16)
    controls = control_map.reshape(blocks, K_DEV, COLS_DEV).astype(jnp.float32)
    gradient = jnp.einsum("bkc,bc->bk", controls, mixed.reshape(blocks, COLS_DEV).astype(jnp.float32), precision=lax.Precision.HIGHEST)
    return adjoint, pressure, sensitivity, gradient.reshape(-1)
```

```python
import jax
import jax.numpy as jnp
from jax import lax
from jax.experimental import pallas as pl
from jax.experimental.pallas import tpu as pltpu
from jax.sharding import PartitionSpec as P

HSWEEPS = 4
diffusion_rate = 0.12
melt_rate = 0.3

TILES = 32
GROUP = 8
CHIPS = 4
COLUMNS = 32768
LAYERS = 20
LANES = 128
ROWS = COLUMNS // LANES
RUN = 10
MSG = 16
EDGE = 8
WIDE = RUN * LANES + LANES
TALL = TILES + 2 * EDGE
CONTROLS = 64
PARTS = 4
PART = ROWS // PARTS
MESH = pl.DeviceIdType.MESH

LEVELS = ((32, 16, 24), (16, 24, 40), (8, 48, 80), (4, 88, 160), (2, 168, 256))


def rows_at(start, count):
    return pl.ds(pl.multiple_of(start, 8), count)


def kernel(
    mix_ref, inverse_ref, cot_hbm, slide_hbm, fric_hbm, thaw_hbm, melt_hbm, store_hbm, owner_hbm, open_hbm, map_hbm,
    press_hbm, sens_hbm, grad_ref,
    cot, cmap, slide, fric, thaw, melt, store, owner, chan, source, basal,
    send1, send2, recv1, recv2, cond, cond_low, cond_high, coef, pressure, press_out, back_send,
    lev0, lev1, lev2, lev3, lev4, sens, gathered, other_send, other_recv, mine,
    load_sem, cot_sem, self_sem, send_sem, recv_sem, part_send, part_recv, pair_send, pair_recv, out_sem,
):
    a = lax.axis_index("col")
    g = lax.axis_index("grp")
    chip = g // 2
    core = lax.rem(g, 2)
    sibling = chip * 2 + (1 - core)
    up = lax.rem(g + GROUP - 1, GROUP)
    down = lax.rem(g + 1, GROUP)
    left = lax.rem(a + TILES - 1, TILES)
    right = lax.rem(a + 1, TILES)

    def load(src, dst, number):
        copy = pltpu.make_async_copy(src, dst, load_sem.at[number])
        copy.start()
        return copy

    owner_load = load(owner_hbm, owner, 0)
    melt_load = load(melt_hbm, melt.at[pl.ds(0, ROWS)], 1)
    store_load = load(store_hbm, store.at[pl.ds(0, ROWS)], 2)
    chan_load = load(open_hbm, chan, 3)
    cot_loads = []
    piece = COLUMNS // PARTS
    for q in range(PARTS):
        copy = pltpu.make_async_copy(
            cot_hbm.at[:, pl.ds(q * piece, piece)], cot.at[:, pl.ds(q * piece, piece)], cot_sem.at[q]
        )
        copy.start()
        cot_loads.append(copy)
    thaw_load = load(thaw_hbm, thaw, 4)
    slide_load = load(slide_hbm, slide, 5)
    fric_load = load(fric_hbm, fric, 6)
    map_load = load(map_hbm, cmap, 7)

    barrier = pltpu.get_barrier_semaphore()

    def greet(d, carry):
        pl.semaphore_signal(
            barrier, inc=1, device_id={"col": lax.rem(a + d, TILES)}, device_id_type=MESH
        )
        return carry

    lax.fori_loop(1, TILES, greet, 0)
    for other in (up, down):
        pl.semaphore_signal(barrier, inc=1, device_id={"grp": other}, device_id_type=MESH)
    for d in range(1, CHIPS):
        same_core = lax.rem(chip + d, CHIPS) * 2 + core
        pl.semaphore_signal(barrier, inc=1, device_id={"grp": same_core}, device_id_type=MESH)

    lane = lax.broadcasted_iota(jnp.int32, (1, LANES), 1)
    edge_rows = jnp.zeros((4 * MSG, LANES), jnp.float32)
    for ref in (recv1, recv2):
        ref[0 : 4 * MSG, :] = edge_rows
        ref[(TALL - 4) * MSG : TALL * MSG, :] = edge_rows

    owner_load.wait()
    owners = owner[...]
    starts = [jnp.int32(0)]
    for t in range(1, TILES):
        below = jnp.where(owners < t, 1.0, 0.0).astype(jnp.float32)
        partial = jnp.sum(below.reshape(ROWS // 8, 8, LANES), axis=0)
        starts.append(jnp.clip(jnp.sum(partial).astype(jnp.int32), 0, COLUMNS))
    starts.append(jnp.int32(COLUMNS))

    slot = lax.broadcasted_iota(jnp.int32, (MSG, LANES), 0) * LANES + lax.broadcasted_iota(
        jnp.int32, (MSG, LANES), 1
    )

    def window(ref, t):
        first = lax.shift_right_logical(starts[t], 7)
        turn = lax.bitwise_and(starts[t], LANES - 1)
        back_turn = lax.bitwise_and(LANES - turn, LANES - 1)
        low = pltpu.roll(ref[pl.ds(first, MSG), :], back_turn, 1)
        high = pltpu.roll(ref[pl.ds(first + 1, MSG), :], back_turn, 1)
        both = jnp.where(lane < LANES - turn, low, high)
        return jnp.where(slot < starts[t + 1] - starts[t], both, 0.0)

    store_load.wait()
    melt_load.wait()
    for t in range(TILES):
        stored = window(store, t)
        melted = window(melt, t)
        send1[MSG * t : MSG * t + RUN, :] = stored[:RUN]
        send1[MSG * t + RUN : MSG * (t + 1), :] = melted[: MSG - RUN]
        send2[MSG * t : MSG * t + 2 * RUN - MSG, :] = melted[MSG - RUN : RUN]

    chan_load.wait()
    cond[EDGE : EDGE + TILES, : RUN * LANES] = jnp.where(chan[...] == 1, diffusion_rate, 0.25 * diffusion_rate)

    pl.semaphore_wait(barrier, TILES - 1 + 2 + CHIPS - 1)

    def post(src, dst, number, where):
        copy = pltpu.make_async_remote_copy(
            src_ref=src, dst_ref=dst, send_sem=send_sem.at[number], recv_sem=recv_sem.at[number],
            device_id=where, device_id_type=MESH,
        )
        copy.start()
        return copy

    def to_all(src, dst, number, self_number):
        def one(d, carry):
            target = lax.rem(a + d, TILES)
            post(src.at[rows_at(target * MSG, MSG)], dst.at[rows_at((EDGE + a) * MSG, MSG)], number, {"col": target})
            return carry

        lax.fori_loop(1, TILES, one, 0)
        own = pltpu.make_async_copy(
            src.at[rows_at(a * MSG, MSG)], dst.at[rows_at((EDGE + a) * MSG, MSG)], self_sem.at[self_number]
        )
        own.start()
        return own

    def all_done(buffer, rows, sem):
        pltpu.make_async_copy(buffer.at[pl.ds(0, rows)], buffer.at[pl.ds(0, rows)], sem).wait()

    chan_low = post(cond.at[EDGE : EDGE + TILES, (RUN - 1) * LANES : RUN * LANES], cond_low, 0, {"col": right})
    chan_high = post(cond.at[EDGE : EDGE + TILES, 0:LANES], cond_high, 1, {"col": left})
    own1 = to_all(send1, recv1, 2, 0)

    weight = jnp.broadcast_to(inverse_ref[:, LAYERS - 1 : LAYERS], (LAYERS, LANES))
    sublane = lax.broadcasted_iota(jnp.int32, (8, LANES), 0)
    thaw_load.wait()
    slide_load.wait()
    fric_load.wait()
    for q in range(PARTS):
        cot_loads[q].wait()

        def last_layer(j, carry):
            block = jnp.zeros((8, LANES), jnp.float32)
            for k in range(8):
                layers = cot[:, pl.ds(pl.multiple_of(j * 1024 + k * LANES, LANES), LANES)]
                total = jnp.sum(layers * weight, axis=0, keepdims=True)
                block = jnp.where(sublane == k, total, block)
            at = rows_at(j * 8, 8)
            base = thaw[at, :].astype(jnp.float32) * slide[at, :] * block
            basal[at, :] = base
            source[at, :] = fric[at, :] * base
            return carry

        lax.fori_loop(q * 8, (q + 1) * 8, last_layer, 0)

    for t in range(TILES):
        send2[MSG * t + 2 * RUN - MSG : MSG * t + 3 * RUN - MSG, :] = window(source, t)[:RUN]

    tile = lax.broadcasted_iota(jnp.int32, (TILES, LANES), 0)
    lanes = lax.broadcasted_iota(jnp.int32, (TILES, LANES), 1)

    def beside(first, last):
        ahead = jnp.where(tile == TILES - 1, 0.0, pltpu.roll(first, TILES - 1, 0))
        behind = jnp.where(tile == 0, 0.0, pltpu.roll(last, 1, 0))
        return jnp.where(lanes < 4, ahead, jnp.where(lanes >= LANES - 4, behind, 0.0))

    def every(ref, row):
        return ref[pl.ds(row, TILES, stride=MSG), :]

    send2[pl.ds(14, TILES, stride=MSG), :] = beside(every(send2, 4), every(send2, 13))
    melt_sides = beside(every(send1, 10), every(send2, 3))
    store_sides = beside(every(send1, 0), every(send1, 9))
    store_moved = jnp.where(
        lanes < 64, pltpu.roll(store_sides, 4, 1), pltpu.roll(store_sides, LANES - 4, 1)
    )
    send2[pl.ds(15, TILES, stride=MSG), :] = jnp.where(
        jnp.logical_or(lanes < 4, lanes >= LANES - 4), melt_sides, store_moved
    )
    own2 = to_all(send2, recv2, 3, 1)

    chan_low.wait_recv()
    chan_high.wait_recv()
    low_side = jnp.where(jnp.logical_and(lanes >= LANES - 4, a > 0), cond_low[...], 0.0)
    cond[EDGE : EDGE + TILES, RUN * LANES :] = jnp.where(
        jnp.logical_and(lanes < 4, a < TILES - 1), cond_high[...], low_side
    )
    chan_up = post(cond.at[pl.ds(EDGE, EDGE)], cond.at[pl.ds(EDGE + TILES, EDGE)], 4, {"grp": up})
    chan_down = post(cond.at[pl.ds(TILES, EDGE)], cond.at[pl.ds(0, EDGE)], 5, {"grp": down})

    def rows_beside(buffer, number):
        first = post(
            buffer.at[pl.ds(EDGE * MSG, 4 * MSG)], buffer.at[pl.ds((EDGE + TILES) * MSG, 4 * MSG)], number, {"grp": up}
        )
        second = post(
            buffer.at[pl.ds((TILES + 4) * MSG, 4 * MSG)], buffer.at[pl.ds(4 * MSG, 4 * MSG)], number + 1, {"grp": down}
        )
        return first, second

    others = (TILES - 1) * MSG
    own1.wait()
    all_done(recv1, others, recv_sem.at[2])
    rows1 = rows_beside(recv1, 6)
    chan_up.wait_recv()
    chan_down.wait_recv()
    for copy in rows1:
        copy.wait_recv()

    row = lax.broadcasted_iota(jnp.int32, (TALL, LANES), 0)
    inside = jnp.logical_and(
        jnp.logical_or(row >= EDGE, g > 0), jnp.logical_or(row < EDGE + TILES, g < GROUP - 1)
    )

    def mesh_rows(ref, k):
        return ref[pl.ds(k, TALL, stride=MSG), :]

    for k in range(RUN):
        at = slice(k * LANES, (k + 1) * LANES)
        coef[:, at] = jnp.where(inside, cond[:, at] / (1.0 + mesh_rows(recv1, k)), 0.0)

    own2.wait()
    all_done(recv2, others, recv_sem.at[3])
    rows2 = rows_beside(recv2, 8)
    for copy in rows2:
        copy.wait_recv()

    side = mesh_rows(recv2, 15)
    lane_tall = lax.broadcasted_iota(jnp.int32, (TALL, LANES), 1)
    store_side = jnp.where(lane_tall < 64, pltpu.roll(side, LANES - 4, 1), pltpu.roll(side, 4, 1))
    used = jnp.logical_or(lane_tall < 4, lane_tall >= LANES - 4)
    store_side = jnp.where(used, store_side, 0.0)
    melt_side = jnp.where(used, side, 0.0)
    at = slice(RUN * LANES, WIDE)
    coef[:, at] = jnp.where(inside, cond[:, at] / (1.0 + store_side), 0.0)
    melts = [mesh_rows(recv1, RUN + k) for k in range(MSG - RUN)]
    melts += [mesh_rows(recv2, k) for k in range(2 * RUN - MSG)] + [melt_side]
    keeps = [1.0 - melt_rate * part for part in melts]
    now = [jnp.where(inside, mesh_rows(recv2, 2 * RUN - MSG + k), 0.0) for k in range(RUN + 1)]
    keep = jnp.concatenate(keeps, axis=1)
    field = jnp.concatenate(now, axis=1)
    pressure[...] = field
    for sweep in range(HSWEEPS):
        field = pressure[...]
        rate = coef[...]
        sides = (
            pltpu.roll(field, 1, 1) + pltpu.roll(field, WIDE - 1, 1) + pltpu.roll(field, 1, 0) + pltpu.roll(field, TALL - 1, 0)
        )
        pressure[...] = keep * field + rate * (sides - 4.0 * field)

    for k in range(RUN):
        for i in range(TILES // 8):
            cells = pressure[EDGE + 8 * i : EDGE + 8 * i + 8, k * LANES : (k + 1) * LANES]
            back_send[pl.ds(8 * i * MSG + k, 8, stride=MSG), :] = cells
    press_out[...] = pressure[EDGE : EDGE + TILES, : RUN * LANES]
    press_copy = pltpu.make_async_copy(press_out, press_hbm, out_sem.at[0])
    press_copy.start()

    pad0 = LEVELS[0][1]

    def give_back(d, carry):
        target = lax.rem(a + d, TILES)
        post(
            back_send.at[rows_at(target * MSG, MSG)], lev0.at[a, pl.ds(pad0, MSG)], 10, {"col": target}
        )
        return carry

    lax.fori_loop(1, TILES, give_back, 0)
    own_back = pltpu.make_async_copy(
        back_send.at[rows_at(a * MSG, MSG)], lev0.at[a, pl.ds(pad0, MSG)], self_sem.at[2]
    )
    own_back.start()
    own_back.wait()
    all_done(back_send, others, recv_sem.at[10])

    levels = (lev0, lev1, lev2, lev3, lev4)
    for level, (nodes, pad, tall) in enumerate(LEVELS):
        ref = levels[level]
        index = lax.broadcasted_iota(jnp.int32, (tall, LANES), 0) * LANES + lax.broadcasted_iota(
            jnp.int32, (tall, LANES), 1
        )
        for node in range(nodes // 2):
            begin = starts[(2 * node) << level]
            length = jnp.clip(starts[(2 * node + 1) << level] - begin, 0, (RUN << level) * LANES)
            first = lax.shift_right_logical(length, 7)
            turn = lax.bitwise_and(length, LANES - 1)
            mine_rows = ref[2 * node, pl.ds(pad, tall), :]
            here = pltpu.roll(ref[2 * node + 1, pl.ds(pad - first, tall), :], turn, 1)
            before = pltpu.roll(ref[2 * node + 1, pl.ds(pad - 1 - first, tall), :], turn, 1)
            moved = jnp.where(lane >= turn, here, before)
            merged = jnp.where(index < length, mine_rows, moved)
            if level < len(LEVELS) - 1:
                levels[level + 1][node, pl.ds(LEVELS[level + 1][1], tall), :] = merged
            else:
                value = thaw[...].astype(jnp.float32) * fric[...] * (basal[...] + merged)
                sens[...] = value

    sens_copy = pltpu.make_async_copy(sens, sens_hbm, out_sem.at[1])
    sens_copy.start()

    parts = []
    for q in range(PARTS):
        for d in range(1, CHIPS):
            same_core = lax.rem(chip + d, CHIPS) * 2 + core
            copy = pltpu.make_async_remote_copy(
                src_ref=sens.at[pl.ds(q * PART, PART)],
                dst_ref=gathered.at[d, pl.ds(q * PART, PART)],
                send_sem=part_send.at[q, d - 1],
                recv_sem=part_recv.at[q, d - 1],
                device_id={"grp": same_core},
                device_id_type=MESH,
            )
            copy.start()
            parts.append(copy)

    def factor(who, d):
        return mix_ref[who, lax.rem(chip + CHIPS - d, CHIPS) * 2 + core]

    to_self = [factor(g, d) for d in range(CHIPS)]
    to_other = [factor(sibling, d) for d in range(CHIPS)]
    pairs = []
    for q in range(PARTS):
        at = pl.ds(q * PART, PART)
        for d in range(CHIPS - 1):
            parts[q * (CHIPS - 1) + d].wait_recv()
        pieces = [sens[at, :]] + [gathered[d, at, :] for d in range(1, CHIPS)]
        other_send[at, :] = sum(to_other[d] * pieces[d] for d in range(CHIPS))
        copy = pltpu.make_async_remote_copy(
            src_ref=other_send.at[at], dst_ref=other_recv.at[at], send_sem=pair_send.at[q], recv_sem=pair_recv.at[q],
            device_id={"grp": sibling}, device_id_type=MESH,
        )
        copy.start()
        pairs.append(copy)
        mine[at, :] = sum(to_self[d] * pieces[d] for d in range(CHIPS))

    map_load.wait()
    total = jnp.zeros((CONTROLS, LANES), jnp.float32)
    for q in range(PARTS):
        pairs[q].wait_recv()

        def product(j, total):
            at = rows_at(j * 8, 8)
            mixed = (mine[at, :] + other_recv[at, :]).astype(jnp.bfloat16).astype(jnp.float32)
            for s in range(8):
                block = cmap[:, pl.ds(pl.multiple_of(j * 1024 + s * LANES, LANES), LANES)]
                total = total + block.astype(jnp.float32) * mixed[s : s + 1, :]
            return total

        total = lax.fori_loop(q * PART // 8, (q + 1) * PART // 8, product, total)
    grad_ref[...] = jnp.sum(total.T, axis=0, keepdims=True)

    chan_low.wait_send()
    chan_high.wait_send()
    chan_up.wait_send()
    chan_down.wait_send()
    for copy in rows1 + rows2:
        copy.wait_send()
    all_done(send1, others, send_sem.at[2])
    all_done(send2, others, send_sem.at[3])
    all_done(back_send, others, send_sem.at[10])
    for copy in parts + pairs:
        copy.wait_send()
    press_copy.wait()
    sens_copy.wait()


def on_device(
    velocity_cotangent,
    vertical_inverse,
    sliding_speed,
    friction_coef,
    thawed_bed,
    basal_melt,
    storage_coef,
    owner_tile,
    channel_open,
    group_mix,
    control_map,
):
    adjoint = jnp.dot(
        vertical_inverse.T,
        velocity_cotangent,
        precision=lax.Precision.HIGHEST,
        preferred_element_type=jnp.float32,
    )
    shaped = [x.reshape(ROWS, LANES) for x in (sliding_speed, friction_coef, thawed_bed, basal_melt, storage_coef, owner_tile)]
    f32 = jnp.float32
    anywhere = pl.BlockSpec(memory_space=pl.ANY)
    vmem = pl.BlockSpec(memory_space=pltpu.VMEM)
    columns = pltpu.VMEM((ROWS, LANES), f32)
    padded = pltpu.VMEM((ROWS + 24, LANES), f32)
    numbers = pltpu.VMEM((ROWS, LANES), jnp.int32)
    messages = pltpu.VMEM(((TILES + 1) * MSG, LANES), f32)
    received = pltpu.VMEM(((TALL + 1) * MSG, LANES), f32)
    field = pltpu.VMEM((TALL, WIDE), f32)
    dma = pltpu.SemaphoreType.DMA
    pressure, sensitivity, gradient = pl.pallas_call(
        kernel,
        out_shape=(
            jax.ShapeDtypeStruct((TILES, RUN * LANES), f32),
            jax.ShapeDtypeStruct((ROWS, LANES), f32),
            jax.ShapeDtypeStruct((1, CONTROLS), f32),
        ),
        in_specs=[pl.BlockSpec(memory_space=pltpu.SMEM), vmem] + [anywhere] * 9,
        out_specs=(anywhere, anywhere, vmem),
        scratch_shapes=[
            pltpu.VMEM((LAYERS, COLUMNS), f32),
            pltpu.VMEM((CONTROLS, COLUMNS), jnp.bfloat16),
            columns, columns, numbers, padded, padded, numbers,
            pltpu.VMEM((TILES, RUN * LANES), jnp.int32),
            padded, columns,
            messages, messages, received, received,
            field, pltpu.VMEM((TILES, LANES), f32), pltpu.VMEM((TILES, LANES), f32),
            field, field, pltpu.VMEM((TILES, RUN * LANES), f32), messages,
        ]
        + [pltpu.VMEM((nodes, pad + tall, LANES), f32) for nodes, pad, tall in LEVELS]
        + [
            columns, pltpu.VMEM((CHIPS, ROWS, LANES), f32), columns, columns, columns,
            dma((8,)), dma((PARTS,)), dma((3,)), dma((11,)), dma((11,)),
            dma((PARTS, CHIPS - 1)), dma((PARTS, CHIPS - 1)), dma((PARTS,)), dma((PARTS,)), dma((2,)),
        ],
        compiler_params=pltpu.CompilerParams(
            collective_id=0, has_side_effects=True, vmem_limit_bytes=48 * 1024 * 1024
        ),
    )(group_mix, vertical_inverse, velocity_cotangent, *shaped, channel_open, control_map)
    return adjoint, pressure, sensitivity.reshape(COLUMNS), gradient.reshape(CONTROLS)


def solution(mesh):
    in_specs = (
        P(None, ("col", "grp")),
        P(),
        P(("col", "grp")),
        P(("col", "grp")),
        P(("col", "grp")),
        P(("col", "grp")),
        P(("col", "grp")),
        P(("col", "grp"), None),
        P("grp", "col"),
        P(),
        P(("col", "grp"), None),
    )
    out_specs = (P(None, ("col", "grp")), P("grp", "col"), P(("col", "grp")), P(("col", "grp")))
    return jax.shard_map(
        on_device, mesh=mesh, in_specs=in_specs, out_specs=out_specs, check_vma=False
    )
```

```python
import functools

import jax
import jax.numpy as jnp
from jax import lax
from jax.experimental import pallas as pl
from jax.experimental.pallas import tpu as pltpu
from jax.sharding import PartitionSpec as P

HSWEEPS = 4
diffusion_rate = 0.12
melt_rate = 0.3

TILES = 32
GROUP = 8
CHIPS = 4
COLUMNS = 32768
LAYERS = 20
LANES = 128
ROWS = COLUMNS // LANES
RUN = 10
MSG = 16
EDGE = 8
WIDE = RUN * LANES + LANES
TALL = TILES + 2 * EDGE
CONTROLS = 64
PARTS = 4
PART = ROWS // PARTS
MESH = pl.DeviceIdType.MESH
VMEM_BYTES = 64 * 1024 * 1024

LEVELS = ((32, 16, 24), (16, 24, 40), (8, 48, 80), (4, 88, 160), (2, 168, 256))


def rows_at(start, count):
    return pl.ds(pl.multiple_of(start, 8), count)


def kernel(
    mix_ref, inverse_ref, cot_hbm, slide_hbm, fric_hbm, thaw_hbm, melt_hbm, store_hbm, owner_hbm, open_hbm, map_hbm,
    press_hbm, sens_hbm, grad_ref,
    cot, cmap, slide, fric, thaw, melt, store, owner, chan, source, basal,
    send1, send2, recv1, recv2, cond, cond_low, cond_high, coef, pressure, press_out, back_send,
    lev0, lev1, lev2, lev3, lev4, sens, gathered, other_send, other_recv, mine,
    load_sem, cot_sem, self_sem, send_sem, recv_sem, part_send, part_recv, pair_send, pair_recv, out_sem,
):
    a = lax.axis_index("col")
    g = lax.axis_index("grp")
    chip = g // 2
    core = lax.rem(g, 2)
    sibling = chip * 2 + (1 - core)
    up = lax.rem(g + GROUP - 1, GROUP)
    down = lax.rem(g + 1, GROUP)
    left = lax.rem(a + TILES - 1, TILES)
    right = lax.rem(a + 1, TILES)

    def load(src, dst, number):
        copy = pltpu.make_async_copy(src, dst, load_sem.at[number])
        copy.start()
        return copy

    owner_load = load(owner_hbm, owner, 0)
    melt_load = load(melt_hbm, melt.at[pl.ds(0, ROWS)], 1)
    store_load = load(store_hbm, store.at[pl.ds(0, ROWS)], 2)
    chan_load = load(open_hbm, chan, 3)
    cot_loads = []
    piece = COLUMNS // PARTS
    for q in range(PARTS):
        copy = pltpu.make_async_copy(
            cot_hbm.at[:, pl.ds(q * piece, piece)], cot.at[:, pl.ds(q * piece, piece)], cot_sem.at[q]
        )
        copy.start()
        cot_loads.append(copy)
    thaw_load = load(thaw_hbm, thaw, 4)
    slide_load = load(slide_hbm, slide, 5)
    fric_load = load(fric_hbm, fric, 6)
    map_load = load(map_hbm, cmap, 7)

    barrier = pltpu.get_barrier_semaphore()

    def greet(d, carry):
        pl.semaphore_signal(
            barrier, inc=1, device_id={"col": lax.rem(a + d, TILES)}, device_id_type=MESH
        )
        return carry

    lax.fori_loop(1, TILES, greet, 0)
    for other in (up, down):
        pl.semaphore_signal(barrier, inc=1, device_id={"grp": other}, device_id_type=MESH)
    for d in range(1, CHIPS):
        same_core = lax.rem(chip + d, CHIPS) * 2 + core
        pl.semaphore_signal(barrier, inc=1, device_id={"grp": same_core}, device_id_type=MESH)

    lane = lax.broadcasted_iota(jnp.int32, (1, LANES), 1)
    edge_rows = jnp.zeros((4 * MSG, LANES), jnp.float32)
    for ref in (recv1, recv2):
        ref[0 : 4 * MSG, :] = edge_rows
        ref[(TALL - 4) * MSG : TALL * MSG, :] = edge_rows

    owner_load.wait()
    owners = owner[...]
    starts = [jnp.int32(0)]
    for t in range(1, TILES):
        below = jnp.where(owners < t, 1.0, 0.0).astype(jnp.float32)
        partial = jnp.sum(below.reshape(ROWS // 8, 8, LANES), axis=0)
        starts.append(jnp.clip(jnp.sum(partial).astype(jnp.int32), 0, COLUMNS))
    starts.append(jnp.int32(COLUMNS))

    slot = lax.broadcasted_iota(jnp.int32, (MSG, LANES), 0) * LANES + lax.broadcasted_iota(
        jnp.int32, (MSG, LANES), 1
    )

    def window(ref, t):
        first = lax.shift_right_logical(starts[t], 7)
        turn = lax.bitwise_and(starts[t], LANES - 1)
        back_turn = lax.bitwise_and(LANES - turn, LANES - 1)
        low = pltpu.roll(ref[pl.ds(first, MSG), :], back_turn, 1)
        high = pltpu.roll(ref[pl.ds(first + 1, MSG), :], back_turn, 1)
        both = jnp.where(lane < LANES - turn, low, high)
        return jnp.where(slot < starts[t + 1] - starts[t], both, 0.0)

    store_load.wait()
    melt_load.wait()
    for t in range(TILES):
        stored = window(store, t)
        melted = window(melt, t)
        send1[MSG * t : MSG * t + RUN, :] = stored[:RUN]
        send1[MSG * t + RUN : MSG * (t + 1), :] = melted[: MSG - RUN]
        send2[MSG * t : MSG * t + 2 * RUN - MSG, :] = melted[MSG - RUN : RUN]

    chan_load.wait()
    cond[EDGE : EDGE + TILES, : RUN * LANES] = jnp.where(chan[...] == 1, diffusion_rate, 0.25 * diffusion_rate)

    pl.semaphore_wait(barrier, TILES - 1 + 2 + CHIPS - 1)

    def post(src, dst, number, where):
        copy = pltpu.make_async_remote_copy(
            src_ref=src, dst_ref=dst, send_sem=send_sem.at[number], recv_sem=recv_sem.at[number],
            device_id=where, device_id_type=MESH,
        )
        copy.start()
        return copy

    def to_all(src, dst, number, self_number):
        def one(d, carry):
            target = lax.rem(a + d, TILES)
            post(src.at[rows_at(target * MSG, MSG)], dst.at[rows_at((EDGE + a) * MSG, MSG)], number, {"col": target})
            return carry

        lax.fori_loop(1, TILES, one, 0)
        own = pltpu.make_async_copy(
            src.at[rows_at(a * MSG, MSG)], dst.at[rows_at((EDGE + a) * MSG, MSG)], self_sem.at[self_number]
        )
        own.start()
        return own

    def all_done(buffer, rows, sem):
        pltpu.make_async_copy(buffer.at[pl.ds(0, rows)], buffer.at[pl.ds(0, rows)], sem).wait()

    chan_low = post(cond.at[EDGE : EDGE + TILES, (RUN - 1) * LANES : RUN * LANES], cond_low, 0, {"col": right})
    chan_high = post(cond.at[EDGE : EDGE + TILES, 0:LANES], cond_high, 1, {"col": left})
    own1 = to_all(send1, recv1, 2, 0)

    weight = jnp.broadcast_to(inverse_ref[:, LAYERS - 1 : LAYERS], (LAYERS, LANES))
    sublane = lax.broadcasted_iota(jnp.int32, (8, LANES), 0)
    thaw_load.wait()
    slide_load.wait()
    fric_load.wait()
    for q in range(PARTS):
        cot_loads[q].wait()

        def last_layer(j, carry):
            block = jnp.zeros((8, LANES), jnp.float32)
            for k in range(8):
                layers = cot[:, pl.ds(pl.multiple_of(j * 1024 + k * LANES, LANES), LANES)]
                total = jnp.sum(layers * weight, axis=0, keepdims=True)
                block = jnp.where(sublane == k, total, block)
            at = rows_at(j * 8, 8)
            base = thaw[at, :].astype(jnp.float32) * slide[at, :] * block
            basal[at, :] = base
            source[at, :] = fric[at, :] * base
            return carry

        lax.fori_loop(q * 8, (q + 1) * 8, last_layer, 0)

    for t in range(TILES):
        send2[MSG * t + 2 * RUN - MSG : MSG * t + 3 * RUN - MSG, :] = window(source, t)[:RUN]

    tile = lax.broadcasted_iota(jnp.int32, (TILES, LANES), 0)
    lanes = lax.broadcasted_iota(jnp.int32, (TILES, LANES), 1)

    def beside(first, last):
        ahead = jnp.where(tile == TILES - 1, 0.0, pltpu.roll(first, TILES - 1, 0))
        behind = jnp.where(tile == 0, 0.0, pltpu.roll(last, 1, 0))
        return jnp.where(lanes < 4, ahead, jnp.where(lanes >= LANES - 4, behind, 0.0))

    def every(ref, row):
        return ref[pl.ds(row, TILES, stride=MSG), :]

    send2[pl.ds(14, TILES, stride=MSG), :] = beside(every(send2, 4), every(send2, 13))
    melt_sides = beside(every(send1, 10), every(send2, 3))
    store_sides = beside(every(send1, 0), every(send1, 9))
    store_moved = jnp.where(
        lanes < 64, pltpu.roll(store_sides, 4, 1), pltpu.roll(store_sides, LANES - 4, 1)
    )
    send2[pl.ds(15, TILES, stride=MSG), :] = jnp.where(
        jnp.logical_or(lanes < 4, lanes >= LANES - 4), melt_sides, store_moved
    )
    own2 = to_all(send2, recv2, 3, 1)

    chan_low.wait_recv()
    chan_high.wait_recv()
    low_side = jnp.where(jnp.logical_and(lanes >= LANES - 4, a > 0), cond_low[...], 0.0)
    cond[EDGE : EDGE + TILES, RUN * LANES :] = jnp.where(
        jnp.logical_and(lanes < 4, a < TILES - 1), cond_high[...], low_side
    )
    chan_up = post(cond.at[pl.ds(EDGE, EDGE)], cond.at[pl.ds(EDGE + TILES, EDGE)], 4, {"grp": up})
    chan_down = post(cond.at[pl.ds(TILES, EDGE)], cond.at[pl.ds(0, EDGE)], 5, {"grp": down})

    def rows_beside(buffer, number):
        first = post(
            buffer.at[pl.ds(EDGE * MSG, 4 * MSG)], buffer.at[pl.ds((EDGE + TILES) * MSG, 4 * MSG)], number, {"grp": up}
        )
        second = post(
            buffer.at[pl.ds((TILES + 4) * MSG, 4 * MSG)], buffer.at[pl.ds(4 * MSG, 4 * MSG)], number + 1, {"grp": down}
        )
        return first, second

    others = (TILES - 1) * MSG
    own1.wait()
    all_done(recv1, others, recv_sem.at[2])
    rows1 = rows_beside(recv1, 6)
    chan_up.wait_recv()
    chan_down.wait_recv()
    for copy in rows1:
        copy.wait_recv()

    row = lax.broadcasted_iota(jnp.int32, (TALL, LANES), 0)
    inside = jnp.logical_and(
        jnp.logical_or(row >= EDGE, g > 0), jnp.logical_or(row < EDGE + TILES, g < GROUP - 1)
    )

    def mesh_rows(ref, k):
        return ref[pl.ds(k, TALL, stride=MSG), :]

    for k in range(RUN):
        at = slice(k * LANES, (k + 1) * LANES)
        coef[:, at] = jnp.where(inside, cond[:, at] / (1.0 + mesh_rows(recv1, k)), 0.0)

    own2.wait()
    all_done(recv2, others, recv_sem.at[3])
    rows2 = rows_beside(recv2, 8)
    for copy in rows2:
        copy.wait_recv()

    side = mesh_rows(recv2, 15)
    lane_tall = lax.broadcasted_iota(jnp.int32, (TALL, LANES), 1)
    store_side = jnp.where(lane_tall < 64, pltpu.roll(side, LANES - 4, 1), pltpu.roll(side, 4, 1))
    used = jnp.logical_or(lane_tall < 4, lane_tall >= LANES - 4)
    store_side = jnp.where(used, store_side, 0.0)
    melt_side = jnp.where(used, side, 0.0)
    at = slice(RUN * LANES, WIDE)
    coef[:, at] = jnp.where(inside, cond[:, at] / (1.0 + store_side), 0.0)
    melts = [mesh_rows(recv1, RUN + k) for k in range(MSG - RUN)]
    melts += [mesh_rows(recv2, k) for k in range(2 * RUN - MSG)] + [melt_side]
    keeps = [1.0 - melt_rate * part for part in melts]
    now = [jnp.where(inside, mesh_rows(recv2, 2 * RUN - MSG + k), 0.0) for k in range(RUN + 1)]
    keep = jnp.concatenate(keeps, axis=1)
    field = jnp.concatenate(now, axis=1)
    pressure[...] = field
    for sweep in range(HSWEEPS):
        field = pressure[...]
        rate = coef[...]
        sides = (
            pltpu.roll(field, 1, 1) + pltpu.roll(field, WIDE - 1, 1) + pltpu.roll(field, 1, 0) + pltpu.roll(field, TALL - 1, 0)
        )
        pressure[...] = keep * field + rate * (sides - 4.0 * field)

    for k in range(RUN):
        for i in range(TILES // 8):
            cells = pressure[EDGE + 8 * i : EDGE + 8 * i + 8, k * LANES : (k + 1) * LANES]
            back_send[pl.ds(8 * i * MSG + k, 8, stride=MSG), :] = cells
    press_out[...] = pressure[EDGE : EDGE + TILES, : RUN * LANES]
    press_copy = pltpu.make_async_copy(press_out, press_hbm, out_sem.at[0])
    press_copy.start()

    pad0 = LEVELS[0][1]

    def give_back(d, carry):
        target = lax.rem(a + d, TILES)
        post(
            back_send.at[rows_at(target * MSG, RUN)], lev0.at[a, pl.ds(pad0, RUN)], 10, {"col": target}
        )
        return carry

    lax.fori_loop(1, TILES, give_back, 0)
    own_back = pltpu.make_async_copy(
        back_send.at[rows_at(a * MSG, RUN)], lev0.at[a, pl.ds(pad0, RUN)], self_sem.at[2]
    )
    own_back.start()
    own_back.wait()
    all_done(back_send, (TILES - 1) * RUN, recv_sem.at[10])

    levels = (lev0, lev1, lev2, lev3, lev4)
    for level, (nodes, pad, tall) in enumerate(LEVELS):
        ref = levels[level]
        index = lax.broadcasted_iota(jnp.int32, (tall, LANES), 0) * LANES + lax.broadcasted_iota(
            jnp.int32, (tall, LANES), 1
        )
        for node in range(nodes // 2):
            begin = starts[(2 * node) << level]
            length = jnp.clip(starts[(2 * node + 1) << level] - begin, 0, (RUN << level) * LANES)
            first = lax.shift_right_logical(length, 7)
            turn = lax.bitwise_and(length, LANES - 1)
            mine_rows = ref[2 * node, pl.ds(pad, tall), :]
            here = pltpu.roll(ref[2 * node + 1, pl.ds(pad - first, tall), :], turn, 1)
            before = pltpu.roll(ref[2 * node + 1, pl.ds(pad - 1 - first, tall), :], turn, 1)
            moved = jnp.where(lane >= turn, here, before)
            merged = jnp.where(index < length, mine_rows, moved)
            if level < len(LEVELS) - 1:
                levels[level + 1][node, pl.ds(LEVELS[level + 1][1], tall), :] = merged
            else:
                value = thaw[...].astype(jnp.float32) * fric[...] * (basal[...] + merged)
                sens[...] = value

    sens_copy = pltpu.make_async_copy(sens, sens_hbm, out_sem.at[1])
    sens_copy.start()

    parts = []
    for q in range(PARTS):
        for d in range(1, CHIPS):
            same_core = lax.rem(chip + d, CHIPS) * 2 + core
            copy = pltpu.make_async_remote_copy(
                src_ref=sens.at[pl.ds(q * PART, PART)],
                dst_ref=gathered.at[d, pl.ds(q * PART, PART)],
                send_sem=part_send.at[q, d - 1],
                recv_sem=part_recv.at[q, d - 1],
                device_id={"grp": same_core},
                device_id_type=MESH,
            )
            copy.start()
            parts.append(copy)

    def factor(who, d):
        return mix_ref[who, lax.rem(chip + CHIPS - d, CHIPS) * 2 + core]

    to_self = [factor(g, d) for d in range(CHIPS)]
    to_other = [factor(sibling, d) for d in range(CHIPS)]
    pairs = []
    for q in range(PARTS):
        at = pl.ds(q * PART, PART)
        for d in range(CHIPS - 1):
            parts[q * (CHIPS - 1) + d].wait_recv()
        pieces = [sens[at, :]] + [gathered[d, at, :] for d in range(1, CHIPS)]
        other_send[at, :] = sum(to_other[d] * pieces[d] for d in range(CHIPS))
        copy = pltpu.make_async_remote_copy(
            src_ref=other_send.at[at], dst_ref=other_recv.at[at], send_sem=pair_send.at[q], recv_sem=pair_recv.at[q],
            device_id={"grp": sibling}, device_id_type=MESH,
        )
        copy.start()
        pairs.append(copy)
        mine[at, :] = sum(to_self[d] * pieces[d] for d in range(CHIPS))

    map_load.wait()
    total = jnp.zeros((CONTROLS, LANES), jnp.float32)
    for q in range(PARTS):
        pairs[q].wait_recv()

        def product(j, total):
            at = rows_at(j * 8, 8)
            mixed = (mine[at, :] + other_recv[at, :]).astype(jnp.bfloat16).astype(jnp.float32)
            for s in range(8):
                block = cmap[:, pl.ds(pl.multiple_of(j * 1024 + s * LANES, LANES), LANES)]
                total = total + block.astype(jnp.float32) * mixed[s : s + 1, :]
            return total

        total = lax.fori_loop(q * PART // 8, (q + 1) * PART // 8, product, total)
    grad_ref[...] = jnp.sum(total.T, axis=0, keepdims=True)

    chan_low.wait_send()
    chan_high.wait_send()
    chan_up.wait_send()
    chan_down.wait_send()
    for copy in rows1 + rows2:
        copy.wait_send()
    all_done(send1, others, send_sem.at[2])
    all_done(send2, others, send_sem.at[3])
    all_done(back_send, (TILES - 1) * RUN, send_sem.at[10])
    for copy in parts + pairs:
        copy.wait_send()
    press_copy.wait()
    sens_copy.wait()


def adjoint_kernel(
    inverse_ref, cot_hbm, press_in, sens_in, grad_in,
    adj_hbm, press_out, sens_out, grad_out,
    cot, adj, in_sem, out_sem, pass_sem,
):
    pieces = in_sem.shape[0]
    width = COLUMNS // pieces
    ins, outs = [], []
    for q in range(pieces):
        at = pl.ds(q * width, width)
        copy = pltpu.make_async_copy(cot_hbm.at[:, at], cot.at[:, at], in_sem.at[q])
        copy.start()
        ins.append(copy)
    for number, (src, dst) in enumerate(((press_in, press_out), (sens_in, sens_out), (grad_in, grad_out))):
        copy = pltpu.make_async_copy(src, dst, pass_sem.at[number])
        copy.start()
        outs.append(copy)
    matrix = inverse_ref[...].T
    high = matrix.astype(jnp.bfloat16)
    low = (matrix - high.astype(jnp.float32)).astype(jnp.bfloat16)
    dot = functools.partial(jnp.dot, preferred_element_type=jnp.float32)
    for q in range(pieces):
        ins[q].wait()
        for start in range(q * width, (q + 1) * width, 1024):
            at = slice(start, start + 1024)
            values = cot[:, at]
            values_high = values.astype(jnp.bfloat16)
            values_low = (values - values_high.astype(jnp.float32)).astype(jnp.bfloat16)
            adj[:, at] = dot(high, values_high) + (dot(high, values_low) + dot(low, values_high))
        at = pl.ds(q * width, width)
        copy = pltpu.make_async_copy(adj.at[:, at], adj_hbm.at[:, at], out_sem.at[q])
        copy.start()
        outs.append(copy)
    for copy in outs:
        copy.wait()


def on_device(
    velocity_cotangent,
    vertical_inverse,
    sliding_speed,
    friction_coef,
    thawed_bed,
    basal_melt,
    storage_coef,
    owner_tile,
    channel_open,
    group_mix,
    control_map,
):
    shaped = [x.reshape(ROWS, LANES) for x in (sliding_speed, friction_coef, thawed_bed, basal_melt, storage_coef, owner_tile)]
    f32 = jnp.float32
    anywhere = pl.BlockSpec(memory_space=pltpu.HBM)
    vmem = pl.BlockSpec(memory_space=pltpu.VMEM)
    columns = pltpu.VMEM((ROWS, LANES), f32)
    padded = pltpu.VMEM((ROWS + 24, LANES), f32)
    numbers = pltpu.VMEM((ROWS, LANES), jnp.int32)
    messages = pltpu.VMEM(((TILES + 1) * MSG, LANES), f32)
    received = pltpu.VMEM(((TALL + 1) * MSG, LANES), f32)
    field = pltpu.VMEM((TALL, WIDE), f32)
    dma = pltpu.SemaphoreType.DMA
    pressure, sensitivity, gradient = pl.pallas_call(
        kernel,
        out_shape=(
            jax.ShapeDtypeStruct((TILES, RUN * LANES), f32),
            jax.ShapeDtypeStruct((ROWS, LANES), f32),
            jax.ShapeDtypeStruct((1, CONTROLS), f32),
        ),
        in_specs=[pl.BlockSpec(memory_space=pltpu.SMEM), vmem] + [anywhere] * 9,
        out_specs=(anywhere, anywhere, vmem),
        scratch_shapes=[
            pltpu.VMEM((LAYERS, COLUMNS), f32),
            pltpu.VMEM((CONTROLS, COLUMNS), jnp.bfloat16),
            columns, columns, numbers, padded, padded, numbers,
            pltpu.VMEM((TILES, RUN * LANES), jnp.int32),
            padded, columns,
            messages, messages, received, received,
            field, pltpu.VMEM((TILES, LANES), f32), pltpu.VMEM((TILES, LANES), f32),
            field, field, pltpu.VMEM((TILES, RUN * LANES), f32), messages,
        ]
        + [pltpu.VMEM((nodes, pad + tall, LANES), f32) for nodes, pad, tall in LEVELS]
        + [
            columns, pltpu.VMEM((CHIPS, ROWS, LANES), f32), columns, columns, columns,
            dma((8,)), dma((PARTS,)), dma((3,)), dma((11,)), dma((11,)),
            dma((PARTS, CHIPS - 1)), dma((PARTS, CHIPS - 1)), dma((PARTS,)), dma((PARTS,)), dma((2,)),
        ],
        compiler_params=pltpu.CompilerParams(
            collective_id=0, has_side_effects=True, vmem_limit_bytes=VMEM_BYTES
        ),
    )(group_mix, vertical_inverse, velocity_cotangent, *shaped, channel_open, control_map)
    adjoint, pressure, sensitivity, gradient = pl.pallas_call(
        adjoint_kernel,
        out_shape=(
            jax.ShapeDtypeStruct((LAYERS, COLUMNS), f32),
            jax.ShapeDtypeStruct((TILES, RUN * LANES), f32),
            jax.ShapeDtypeStruct((ROWS, LANES), f32),
            jax.ShapeDtypeStruct((1, CONTROLS), f32),
        ),
        in_specs=[vmem] + [anywhere] * 4,
        out_specs=(anywhere,) * 4,
        scratch_shapes=[
            pltpu.VMEM((LAYERS, COLUMNS), f32), pltpu.VMEM((LAYERS, COLUMNS), f32), dma((8,)), dma((8,)), dma((3,)),
        ],
        compiler_params=pltpu.CompilerParams(vmem_limit_bytes=VMEM_BYTES),
    )(vertical_inverse, velocity_cotangent, pressure, sensitivity, gradient)
    return adjoint, pressure, sensitivity.reshape(COLUMNS), gradient.reshape(CONTROLS)


def solution(mesh):
    in_specs = (
        P(None, ("col", "grp")),
        P(),
        P(("col", "grp")),
        P(("col", "grp")),
        P(("col", "grp")),
        P(("col", "grp")),
        P(("col", "grp")),
        P(("col", "grp"), None),
        P("grp", "col"),
        P(),
        P(("col", "grp"), None),
    )
    out_specs = (P(None, ("col", "grp")), P("grp", "col"), P(("col", "grp")), P(("col", "grp")))
    return jax.shard_map(
        on_device, mesh=mesh, in_specs=in_specs, out_specs=out_specs, check_vma=False
    )
```

```python
import functools

import jax
import jax.numpy as jnp
from jax import lax
from jax.experimental import pallas as pl
from jax.experimental.pallas import tpu as pltpu
from jax.sharding import PartitionSpec as P

HSWEEPS = 4
diffusion_rate = 0.12
melt_rate = 0.3

TILES = 32
GROUP = 8
CHIPS = 4
RING_Y, RING_Z = 4, 8
COLUMNS = 32768
LAYERS = 20
LAYER_ROWS = 24
LANES = 128
ROWS = COLUMNS // LANES
RUN = 10
MSG = 16
EDGE = 8
WIDE = RUN * LANES + LANES
TALL = TILES + 2 * EDGE
CONTROLS = 64
PIECES = 4
AHEAD = 4
PARTS = 4
PART = ROWS // PARTS
MESH = pl.DeviceIdType.MESH
VMEM_BYTES = 64 * 1024 * 1024

LEVELS = ((32, 16, 24), (16, 24, 40), (8, 48, 80), (4, 88, 160), (2, 168, 256))


def rows_at(start, count):
    return pl.ds(pl.multiple_of(start, 8), count)


def kernel(
    mix_ref, inverse_ref, cot_hbm, slide_hbm, fric_hbm, thaw_hbm, melt_hbm, store_hbm, owner_hbm, open_hbm, map_hbm,
    press_hbm, sens_hbm, grad_ref,
    cot, cmap, slide, fric, thaw, melt, store, owner, chan, source, basal,
    send1, send2, recv1, recv2, cond, cond_low, cond_high, coef, pressure, press_out, back_send,
    lev0, lev1, lev2, lev3, lev4, sens, gathered, other_send, other_recv, mine,
    load_sem, cot_sem, self_sem, send_sem, recv_sem, part_send, part_recv, pair_send, pair_recv, out_sem,
):
    a = lax.axis_index("col")
    g = lax.axis_index("grp")
    chip = g // 2
    core = lax.rem(g, 2)
    sibling = chip * 2 + (1 - core)
    up = lax.rem(g + GROUP - 1, GROUP)
    down = lax.rem(g + 1, GROUP)
    left = lax.rem(a + TILES - 1, TILES)
    right = lax.rem(a + 1, TILES)

    def load(src, dst, number):
        copy = pltpu.make_async_copy(src, dst, load_sem.at[number])
        copy.start()
        return copy

    owner_load = load(owner_hbm, owner, 0)
    melt_load = load(melt_hbm, melt.at[pl.ds(0, ROWS)], 1)
    store_load = load(store_hbm, store.at[pl.ds(0, ROWS)], 2)
    chan_load = load(open_hbm, chan, 3)
    cot_loads = []
    piece = COLUMNS // PARTS
    for q in range(PARTS):
        copy = pltpu.make_async_copy(
            cot_hbm.at[:, pl.ds(q * piece, piece)], cot.at[:, pl.ds(q * piece, piece)], cot_sem.at[q]
        )
        copy.start()
        cot_loads.append(copy)
    thaw_load = load(thaw_hbm, thaw, 4)
    slide_load = load(slide_hbm, slide, 5)
    fric_load = load(fric_hbm, fric, 6)
    map_load = load(map_hbm, cmap, 7)

    barrier = pltpu.get_barrier_semaphore()

    def greet(d, carry):
        pl.semaphore_signal(
            barrier, inc=1, device_id={"col": lax.rem(a + d, TILES)}, device_id_type=MESH
        )
        return carry

    lax.fori_loop(1, TILES, greet, 0)
    for other in (up, down):
        pl.semaphore_signal(barrier, inc=1, device_id={"grp": other}, device_id_type=MESH)
    for d in (1, CHIPS - 1):
        same_core = lax.rem(chip + d, CHIPS) * 2 + core
        pl.semaphore_signal(barrier, inc=1, device_id={"grp": same_core}, device_id_type=MESH)

    lane = lax.broadcasted_iota(jnp.int32, (1, LANES), 1)
    edge_rows = jnp.zeros((4 * MSG, LANES), jnp.float32)
    for ref in (recv1, recv2):
        ref[0 : 4 * MSG, :] = edge_rows
        ref[(TALL - 4) * MSG : TALL * MSG, :] = edge_rows

    owner_load.wait()
    owners = owner[...]
    starts = [jnp.int32(0)]
    for t in range(1, TILES):
        below = jnp.where(owners < t, 1.0, 0.0).astype(jnp.float32)
        partial = jnp.sum(below.reshape(ROWS // 8, 8, LANES), axis=0)
        starts.append(jnp.clip(jnp.sum(partial).astype(jnp.int32), 0, COLUMNS))
    starts.append(jnp.int32(COLUMNS))

    slot = lax.broadcasted_iota(jnp.int32, (MSG, LANES), 0) * LANES + lax.broadcasted_iota(
        jnp.int32, (MSG, LANES), 1
    )

    def window(ref, t):
        first = lax.shift_right_logical(starts[t], 7)
        turn = lax.bitwise_and(starts[t], LANES - 1)
        back_turn = lax.bitwise_and(LANES - turn, LANES - 1)
        low = pltpu.roll(ref[pl.ds(first, MSG), :], back_turn, 1)
        high = pltpu.roll(ref[pl.ds(first + 1, MSG), :], back_turn, 1)
        both = jnp.where(lane < LANES - turn, low, high)
        return jnp.where(slot < starts[t + 1] - starts[t], both, 0.0)

    store_load.wait()
    melt_load.wait()
    for t in range(TILES):
        stored = window(store, t)
        melted = window(melt, t)
        send1[MSG * t : MSG * t + RUN, :] = stored[:RUN]
        send1[MSG * t + RUN : MSG * (t + 1), :] = melted[: MSG - RUN]
        send2[MSG * t : MSG * t + 2 * RUN - MSG, :] = melted[MSG - RUN : RUN]

    chan_load.wait()
    cond[EDGE : EDGE + TILES, : RUN * LANES] = jnp.where(chan[...] == 1, diffusion_rate, 0.25 * diffusion_rate)

    pl.semaphore_wait(barrier, TILES - 1 + 2 + 2)

    def post(src, dst, number, where):
        copy = pltpu.make_async_remote_copy(
            src_ref=src, dst_ref=dst, send_sem=send_sem.at[number], recv_sem=recv_sem.at[number],
            device_id=where, device_id_type=MESH,
        )
        copy.start()
        return copy

    def outward(far, order):
        return far + (1 - 2 * lax.rem(order, 2)) * ((order + 1) // 2)

    def far_first(order):
        away_z = outward(RING_Z // 2, order // RING_Y)
        away_y = outward(RING_Y // 2, lax.rem(order, RING_Y))
        return lax.rem(a // RING_Z + away_y, RING_Y) * RING_Z + lax.rem(a + away_z, RING_Z)

    def to_all(src, dst, number, self_number):
        def one(order, carry):
            target = far_first(order)
            post(src.at[rows_at(target * MSG, MSG)], dst.at[rows_at((EDGE + a) * MSG, MSG)], number, {"col": target})
            return carry

        lax.fori_loop(0, TILES - 1, one, 0)
        own = pltpu.make_async_copy(
            src.at[rows_at(a * MSG, MSG)], dst.at[rows_at((EDGE + a) * MSG, MSG)], self_sem.at[self_number]
        )
        own.start()
        return own

    def all_done(buffer, rows, sem):
        pltpu.make_async_copy(buffer.at[pl.ds(0, rows)], buffer.at[pl.ds(0, rows)], sem).wait()

    chan_low = post(cond.at[EDGE : EDGE + TILES, (RUN - 1) * LANES : RUN * LANES], cond_low, 0, {"col": right})
    chan_high = post(cond.at[EDGE : EDGE + TILES, 0:LANES], cond_high, 1, {"col": left})
    own1 = to_all(send1, recv1, 2, 0)

    weight = jnp.broadcast_to(inverse_ref[:, LAYERS - 1 : LAYERS], (LAYERS, LANES))
    sublane = lax.broadcasted_iota(jnp.int32, (8, LANES), 0)
    thaw_load.wait()
    slide_load.wait()
    fric_load.wait()
    for q in range(PARTS):
        cot_loads[q].wait()

        def last_layer(j, carry):
            block = jnp.zeros((8, LANES), jnp.float32)
            for k in range(8):
                layers = cot[:, pl.ds(pl.multiple_of(j * 1024 + k * LANES, LANES), LANES)]
                total = jnp.sum(layers * weight, axis=0, keepdims=True)
                block = jnp.where(sublane == k, total, block)
            at = rows_at(j * 8, 8)
            base = thaw[at, :].astype(jnp.float32) * slide[at, :] * block
            basal[at, :] = base
            source[at, :] = fric[at, :] * base
            return carry

        lax.fori_loop(q * 8, (q + 1) * 8, last_layer, 0)

    for t in range(TILES):
        send2[MSG * t + 2 * RUN - MSG : MSG * t + 3 * RUN - MSG, :] = window(source, t)[:RUN]

    tile = lax.broadcasted_iota(jnp.int32, (TILES, LANES), 0)
    lanes = lax.broadcasted_iota(jnp.int32, (TILES, LANES), 1)

    def beside(first, last):
        ahead = jnp.where(tile == TILES - 1, 0.0, pltpu.roll(first, TILES - 1, 0))
        behind = jnp.where(tile == 0, 0.0, pltpu.roll(last, 1, 0))
        return jnp.where(lanes < 4, ahead, jnp.where(lanes >= LANES - 4, behind, 0.0))

    def every(ref, row):
        return ref[pl.ds(row, TILES, stride=MSG), :]

    send2[pl.ds(14, TILES, stride=MSG), :] = beside(every(send2, 4), every(send2, 13))
    melt_sides = beside(every(send1, 10), every(send2, 3))
    store_sides = beside(every(send1, 0), every(send1, 9))
    store_moved = jnp.where(
        lanes < 64, pltpu.roll(store_sides, 4, 1), pltpu.roll(store_sides, LANES - 4, 1)
    )
    send2[pl.ds(15, TILES, stride=MSG), :] = jnp.where(
        jnp.logical_or(lanes < 4, lanes >= LANES - 4), melt_sides, store_moved
    )
    own2 = to_all(send2, recv2, 3, 1)

    chan_low.wait_recv()
    chan_high.wait_recv()
    low_side = jnp.where(jnp.logical_and(lanes >= LANES - 4, a > 0), cond_low[...], 0.0)
    cond[EDGE : EDGE + TILES, RUN * LANES :] = jnp.where(
        jnp.logical_and(lanes < 4, a < TILES - 1), cond_high[...], low_side
    )
    chan_up = post(cond.at[pl.ds(EDGE, EDGE)], cond.at[pl.ds(EDGE + TILES, EDGE)], 4, {"grp": up})
    chan_down = post(cond.at[pl.ds(TILES, EDGE)], cond.at[pl.ds(0, EDGE)], 5, {"grp": down})

    def rows_beside(buffer, number):
        first = post(
            buffer.at[pl.ds(EDGE * MSG, 4 * MSG)], buffer.at[pl.ds((EDGE + TILES) * MSG, 4 * MSG)], number, {"grp": up}
        )
        second = post(
            buffer.at[pl.ds((TILES + 4) * MSG, 4 * MSG)], buffer.at[pl.ds(4 * MSG, 4 * MSG)], number + 1, {"grp": down}
        )
        return first, second

    others = (TILES - 1) * MSG
    own1.wait()
    all_done(recv1, others, recv_sem.at[2])
    rows1 = rows_beside(recv1, 6)
    chan_up.wait_recv()
    chan_down.wait_recv()
    for copy in rows1:
        copy.wait_recv()

    row = lax.broadcasted_iota(jnp.int32, (TALL, LANES), 0)
    inside = jnp.logical_and(
        jnp.logical_or(row >= EDGE, g > 0), jnp.logical_or(row < EDGE + TILES, g < GROUP - 1)
    )

    def mesh_rows(ref, k):
        return ref[pl.ds(k, TALL, stride=MSG), :]

    for k in range(RUN):
        at = slice(k * LANES, (k + 1) * LANES)
        coef[:, at] = jnp.where(inside, cond[:, at] / (1.0 + mesh_rows(recv1, k)), 0.0)

    own2.wait()
    all_done(recv2, others, recv_sem.at[3])
    rows2 = rows_beside(recv2, 8)
    for copy in rows2:
        copy.wait_recv()

    side = mesh_rows(recv2, 15)
    lane_tall = lax.broadcasted_iota(jnp.int32, (TALL, LANES), 1)
    store_side = jnp.where(lane_tall < 64, pltpu.roll(side, LANES - 4, 1), pltpu.roll(side, 4, 1))
    used = jnp.logical_or(lane_tall < 4, lane_tall >= LANES - 4)
    store_side = jnp.where(used, store_side, 0.0)
    melt_side = jnp.where(used, side, 0.0)
    at = slice(RUN * LANES, WIDE)
    coef[:, at] = jnp.where(inside, cond[:, at] / (1.0 + store_side), 0.0)
    melts = [mesh_rows(recv1, RUN + k) for k in range(MSG - RUN)]
    melts += [mesh_rows(recv2, k) for k in range(2 * RUN - MSG)] + [melt_side]
    keeps = [1.0 - melt_rate * part for part in melts]
    now = [jnp.where(inside, mesh_rows(recv2, 2 * RUN - MSG + k), 0.0) for k in range(RUN + 1)]
    keep = jnp.concatenate(keeps, axis=1)
    field = jnp.concatenate(now, axis=1)
    pressure[...] = field
    for sweep in range(HSWEEPS):
        field = pressure[...]
        rate = coef[...]
        sides = (
            pltpu.roll(field, 1, 1) + pltpu.roll(field, WIDE - 1, 1) + pltpu.roll(field, 1, 0) + pltpu.roll(field, TALL - 1, 0)
        )
        pressure[...] = keep * field + rate * (sides - 4.0 * field)

    for k in range(RUN):
        for i in range(TILES // 8):
            cells = pressure[EDGE + 8 * i : EDGE + 8 * i + 8, k * LANES : (k + 1) * LANES]
            back_send[pl.ds(8 * i * MSG + k, 8, stride=MSG), :] = cells
    press_out[...] = pressure[EDGE : EDGE + TILES, : RUN * LANES]
    press_copy = pltpu.make_async_copy(press_out, press_hbm, out_sem.at[0])
    press_copy.start()

    pad0 = LEVELS[0][1]

    def give_back(order, carry):
        target = far_first(order)
        post(
            back_send.at[rows_at(target * MSG, RUN)], lev0.at[a, pl.ds(pad0, RUN)], 10, {"col": target}
        )
        return carry

    lax.fori_loop(0, TILES - 1, give_back, 0)
    own_back = pltpu.make_async_copy(
        back_send.at[rows_at(a * MSG, RUN)], lev0.at[a, pl.ds(pad0, RUN)], self_sem.at[2]
    )
    own_back.start()
    own_back.wait()
    all_done(back_send, (TILES - 1) * RUN, recv_sem.at[10])

    levels = (lev0, lev1, lev2, lev3, lev4)
    for level, (nodes, pad, tall) in enumerate(LEVELS):
        ref = levels[level]
        index = lax.broadcasted_iota(jnp.int32, (tall, LANES), 0) * LANES + lax.broadcasted_iota(
            jnp.int32, (tall, LANES), 1
        )
        for node in range(nodes // 2):
            begin = starts[(2 * node) << level]
            length = jnp.clip(starts[(2 * node + 1) << level] - begin, 0, (RUN << level) * LANES)
            first = lax.shift_right_logical(length, 7)
            turn = lax.bitwise_and(length, LANES - 1)
            mine_rows = ref[2 * node, pl.ds(pad, tall), :]
            here = pltpu.roll(ref[2 * node + 1, pl.ds(pad - first, tall), :], turn, 1)
            before = pltpu.roll(ref[2 * node + 1, pl.ds(pad - 1 - first, tall), :], turn, 1)
            moved = jnp.where(lane >= turn, here, before)
            merged = jnp.where(index < length, mine_rows, moved)
            if level < len(LEVELS) - 1:
                levels[level + 1][node, pl.ds(LEVELS[level + 1][1], tall), :] = merged
            else:
                value = thaw[...].astype(jnp.float32) * fric[...] * (basal[...] + merged)
                sens[...] = value

    sens_copy = pltpu.make_async_copy(sens, sens_hbm, out_sem.at[1])
    sens_copy.start()

    def pass_on(q, slot, src, ahead):
        copy = pltpu.make_async_remote_copy(
            src_ref=src.at[pl.ds(q * PART, PART)],
            dst_ref=gathered.at[slot, pl.ds(q * PART, PART)],
            send_sem=part_send.at[q, slot - 1],
            recv_sem=part_recv.at[q, slot - 1],
            device_id={"grp": lax.rem(chip + ahead, CHIPS) * 2 + core},
            device_id_type=MESH,
        )
        copy.start()
        return copy

    parts = {}
    for q in range(PARTS):
        parts[q, 1] = pass_on(q, 1, sens, 1)
        other = (q + PARTS // 2) % PARTS
        parts[other, 3] = pass_on(other, 3, sens, CHIPS - 1)
    in_order = []
    for q in range(PARTS // 2):
        other = q + PARTS // 2
        parts[q, 1].wait_recv()
        parts[q, 2] = pass_on(q, 2, gathered.at[1], 1)
        parts[other, 3].wait_recv()
        parts[other, 2] = pass_on(other, 2, gathered.at[3], CHIPS - 1)
        in_order += [q, other]

    def factor(who, d):
        return mix_ref[who, lax.rem(chip + CHIPS - d, CHIPS) * 2 + core]

    to_self = [factor(g, d) for d in range(CHIPS)]
    to_other = [factor(sibling, d) for d in range(CHIPS)]
    pairs = {}
    for q in in_order:
        at = pl.ds(q * PART, PART)
        parts[q, 3 if q < PARTS // 2 else 1].wait_recv()
        parts[q, 2].wait_recv()
        pieces = [sens[at, :]] + [gathered[d, at, :] for d in range(1, CHIPS)]
        other_send[at, :] = sum(to_other[d] * pieces[d] for d in range(CHIPS))
        copy = pltpu.make_async_remote_copy(
            src_ref=other_send.at[at], dst_ref=other_recv.at[at], send_sem=pair_send.at[q], recv_sem=pair_recv.at[q],
            device_id={"grp": sibling}, device_id_type=MESH,
        )
        copy.start()
        pairs[q] = copy
        mine[at, :] = sum(to_self[d] * pieces[d] for d in range(CHIPS))

    map_load.wait()
    total = jnp.zeros((CONTROLS, LANES), jnp.float32)
    for q in in_order:
        pairs[q].wait_recv()

        def product(j, total):
            at = rows_at(j * 8, 8)
            mixed = (mine[at, :] + other_recv[at, :]).astype(jnp.bfloat16).astype(jnp.float32)
            for s in range(8):
                block = cmap[:, pl.ds(pl.multiple_of(j * 1024 + s * LANES, LANES), LANES)]
                total = total + block.astype(jnp.float32) * mixed[s : s + 1, :]
            return total

        total = lax.fori_loop(q * PART // 8, (q + 1) * PART // 8, product, total)
    grad_ref[...] = jnp.sum(total.T, axis=0, keepdims=True)

    chan_low.wait_send()
    chan_high.wait_send()
    chan_up.wait_send()
    chan_down.wait_send()
    for copy in rows1 + rows2:
        copy.wait_send()
    all_done(send1, others, send_sem.at[2])
    all_done(send2, others, send_sem.at[3])
    all_done(back_send, (TILES - 1) * RUN, send_sem.at[10])
    for copy in list(parts.values()) + list(pairs.values()):
        copy.wait_send()
    press_copy.wait()
    sens_copy.wait()


def adjoint_kernel(
    inverse_ref, cot_hbm, press_in, sens_in, grad_in,
    adj_hbm, press_out, sens_out, grad_out,
    cot, adj, press, sens, grad, in_sem, out_sem, pass_sem,
):
    pieces = in_sem.shape[0]
    width = COLUMNS // pieces
    outs, passes = [], []
    for number, (src, dst) in enumerate(((press_in, press), (sens_in, sens), (grad_in, grad))):
        copy = pltpu.make_async_copy(src, dst, pass_sem.at[number])
        copy.start()
        passes.append(copy)
    ins = [
        pltpu.make_async_copy(
            cot_hbm.at[:, pl.ds(q * width, width)], cot.at[:, pl.ds(q * width, width)], in_sem.at[q]
        )
        for q in range(pieces)
    ]
    for copy in ins[:AHEAD]:
        copy.start()
    tall = 8 * LAYER_ROWS
    half = jnp.bfloat16
    dot = functools.partial(jnp.dot, preferred_element_type=jnp.float32)
    layer = lax.rem(lax.broadcasted_iota(jnp.int32, (tall, LAYERS), 0), LAYER_ROWS)
    spread = (layer == lax.broadcasted_iota(jnp.int32, (tall, LAYERS), 1)).astype(jnp.float32).astype(half)
    block = lax.broadcasted_iota(jnp.int32, (tall, tall), 0) // LAYER_ROWS
    own_block = block == lax.broadcasted_iota(jnp.int32, (tall, tall), 1) // LAYER_ROWS

    def diagonal(part):
        rows = dot(spread, part).astype(half)
        full = lax.dot_general(rows, spread, (((1,), (1,)), ((), ())), preferred_element_type=jnp.float32)
        return jnp.where(own_block, full, 0.0).astype(half)

    matrix = inverse_ref[...].T
    matrix_high = matrix.astype(half)
    high = diagonal(matrix_high)
    low = diagonal((matrix - matrix_high.astype(jnp.float32)).astype(half))
    pad = jnp.zeros((LAYER_ROWS - LAYERS, 2 * LANES), jnp.float32)
    step = 16 * LANES
    for q in range(pieces):
        ins[q].wait()
        if q + AHEAD < pieces:
            ins[q + AHEAD].start()
        for start in range(q * width, (q + 1) * width, step):
            tiles = []
            for k in range(8):
                tiles += [cot[:, start + 2 * k * LANES : start + 2 * (k + 1) * LANES], pad]
            values = jnp.concatenate(tiles, axis=0)
            values_high = values.astype(half)
            values_low = (values - values_high.astype(jnp.float32)).astype(half)
            result = dot(high, values_high) + (dot(high, values_low) + dot(low, values_high))
            for k in range(8):
                adj[:, start + 2 * k * LANES : start + 2 * (k + 1) * LANES] = result[
                    k * LAYER_ROWS : k * LAYER_ROWS + LAYERS
                ]
        at = pl.ds(q * width, width)
        copy = pltpu.make_async_copy(adj.at[:, at], adj_hbm.at[:, at], out_sem.at[q])
        copy.start()
        outs.append(copy)
        if q == 0:
            for number, (src, dst) in enumerate(((press, press_out), (sens, sens_out), (grad, grad_out))):
                passes[number].wait()
                copy = pltpu.make_async_copy(src, dst, pass_sem.at[number])
                copy.start()
                outs.append(copy)
    for copy in outs:
        copy.wait()


def on_device(
    velocity_cotangent,
    vertical_inverse,
    sliding_speed,
    friction_coef,
    thawed_bed,
    basal_melt,
    storage_coef,
    owner_tile,
    channel_open,
    group_mix,
    control_map,
):
    shaped = [x.reshape(ROWS, LANES) for x in (sliding_speed, friction_coef, thawed_bed, basal_melt, storage_coef, owner_tile)]
    f32 = jnp.float32
    anywhere = pl.BlockSpec(memory_space=pltpu.HBM)
    vmem = pl.BlockSpec(memory_space=pltpu.VMEM)
    columns = pltpu.VMEM((ROWS, LANES), f32)
    padded = pltpu.VMEM((ROWS + 24, LANES), f32)
    numbers = pltpu.VMEM((ROWS, LANES), jnp.int32)
    messages = pltpu.VMEM(((TILES + 1) * MSG, LANES), f32)
    received = pltpu.VMEM(((TALL + 1) * MSG, LANES), f32)
    field = pltpu.VMEM((TALL, WIDE), f32)
    dma = pltpu.SemaphoreType.DMA
    pressure, sensitivity, gradient = pl.pallas_call(
        kernel,
        out_shape=(
            jax.ShapeDtypeStruct((TILES, RUN * LANES), f32),
            jax.ShapeDtypeStruct((ROWS, LANES), f32),
            jax.ShapeDtypeStruct((1, CONTROLS), f32),
        ),
        in_specs=[pl.BlockSpec(memory_space=pltpu.SMEM), vmem] + [anywhere] * 9,
        out_specs=(anywhere, anywhere, vmem),
        scratch_shapes=[
            pltpu.VMEM((LAYERS, COLUMNS), f32),
            pltpu.VMEM((CONTROLS, COLUMNS), jnp.bfloat16),
            columns, columns, numbers, padded, padded, numbers,
            pltpu.VMEM((TILES, RUN * LANES), jnp.int32),
            padded, columns,
            messages, messages, received, received,
            field, pltpu.VMEM((TILES, LANES), f32), pltpu.VMEM((TILES, LANES), f32),
            field, field, pltpu.VMEM((TILES, RUN * LANES), f32), messages,
        ]
        + [pltpu.VMEM((nodes, pad + tall, LANES), f32) for nodes, pad, tall in LEVELS]
        + [
            columns, pltpu.VMEM((CHIPS, ROWS, LANES), f32), columns, columns, columns,
            dma((8,)), dma((PARTS,)), dma((3,)), dma((11,)), dma((11,)),
            dma((PARTS, CHIPS - 1)), dma((PARTS, CHIPS - 1)), dma((PARTS,)), dma((PARTS,)), dma((2,)),
        ],
        compiler_params=pltpu.CompilerParams(
            collective_id=0, has_side_effects=True, vmem_limit_bytes=VMEM_BYTES
        ),
    )(group_mix, vertical_inverse, velocity_cotangent, *shaped, channel_open, control_map)
    adjoint, pressure, sensitivity, gradient = pl.pallas_call(
        adjoint_kernel,
        out_shape=(
            jax.ShapeDtypeStruct((LAYERS, COLUMNS), f32),
            jax.ShapeDtypeStruct((TILES, RUN * LANES), f32),
            jax.ShapeDtypeStruct((ROWS, LANES), f32),
            jax.ShapeDtypeStruct((1, CONTROLS), f32),
        ),
        in_specs=[vmem] + [anywhere] * 4,
        out_specs=(anywhere,) * 4,
        scratch_shapes=[
            pltpu.VMEM((LAYERS, COLUMNS), f32), pltpu.VMEM((LAYERS, COLUMNS), f32),
            pltpu.VMEM((TILES, RUN * LANES), f32), columns, pltpu.VMEM((1, CONTROLS), f32),
            dma((PIECES,)), dma((PIECES,)), dma((3,)),
        ],
        compiler_params=pltpu.CompilerParams(vmem_limit_bytes=VMEM_BYTES),
    )(vertical_inverse, velocity_cotangent, pressure, sensitivity, gradient)
    return adjoint, pressure, sensitivity.reshape(COLUMNS), gradient.reshape(CONTROLS)


def solution(mesh):
    in_specs = (
        P(None, ("col", "grp")),
        P(),
        P(("col", "grp")),
        P(("col", "grp")),
        P(("col", "grp")),
        P(("col", "grp")),
        P(("col", "grp")),
        P(("col", "grp"), None),
        P("grp", "col"),
        P(),
        P(("col", "grp"), None),
    )
    out_specs = (P(None, ("col", "grp")), P("grp", "col"), P(("col", "grp")), P(("col", "grp")))
    return jax.shard_map(
        on_device, mesh=mesh, in_specs=in_specs, out_specs=out_specs, check_vma=False
    )
```

```python
import functools

import jax
import jax.numpy as jnp
from jax import lax
from jax.experimental import pallas as pl
from jax.experimental.pallas import tpu as pltpu
from jax.sharding import PartitionSpec as P

HSWEEPS = 4
diffusion_rate = 0.12
melt_rate = 0.3

TILES = 32
GROUP = 8
CHIPS = 4
RING_Y, RING_Z = 4, 8
COLUMNS = 32768
LAYERS = 20
LAYER_ROWS = 24
LANES = 128
ROWS = COLUMNS // LANES
RUN = 10
MSG = 16
EDGE = 8
WIDE = RUN * LANES + LANES
TALL = TILES + 2 * EDGE
CONTROLS = 64
PIECES = 4
PARTS = 4
PART = ROWS // PARTS
MESH = pl.DeviceIdType.MESH
VMEM_BYTES = 64 * 1024 * 1024

LEVELS = ((32, 16, 24), (16, 24, 40), (8, 48, 80), (4, 88, 160), (2, 168, 256))


def rows_at(start, count):
    return pl.ds(pl.multiple_of(start, 8), count)


def kernel(
    mix_ref, inverse_ref, cot_hbm, slide_hbm, fric_hbm, thaw_hbm, melt_hbm, store_hbm, owner_hbm, open_hbm, map_hbm,
    adj_hbm, press_hbm, sens_hbm, grad_ref,
    cot, adj, cmap, slide, fric, thaw, melt, store, owner, chan, source, basal,
    send1, send2, recv1, recv2, cond, cond_low, cond_high, coef, pressure, press_out, back_send,
    lev0, lev1, lev2, lev3, lev4, sens, gathered, other_send, other_recv, mine,
    begins, load_sem, cot_sem, self_sem, send_sem, recv_sem, part_send, part_recv, pair_send, pair_recv, out_sem,
):
    a = lax.axis_index("col")
    g = lax.axis_index("grp")
    chip = g // 2
    core = lax.rem(g, 2)
    sibling = chip * 2 + (1 - core)
    up = lax.rem(g + GROUP - 1, GROUP)
    down = lax.rem(g + 1, GROUP)
    left = lax.rem(a + TILES - 1, TILES)
    right = lax.rem(a + 1, TILES)

    def load(src, dst, number):
        copy = pltpu.make_async_copy(src, dst, load_sem.at[number])
        copy.start()
        return copy

    owner_load = load(owner_hbm, owner, 0)
    melt_load = load(melt_hbm, melt.at[pl.ds(0, ROWS)], 1)
    store_load = load(store_hbm, store.at[pl.ds(0, ROWS)], 2)
    barrier = pltpu.get_barrier_semaphore()

    def greet(d, carry):
        pl.semaphore_signal(
            barrier, inc=1, device_id={"col": lax.rem(a + d, TILES)}, device_id_type=MESH
        )
        return carry

    lax.fori_loop(1, TILES, greet, 0)
    for other in (up, down):
        pl.semaphore_signal(barrier, inc=1, device_id={"grp": other}, device_id_type=MESH)
    for d in (1, CHIPS - 1):
        same_core = lax.rem(chip + d, CHIPS) * 2 + core
        pl.semaphore_signal(barrier, inc=1, device_id={"grp": same_core}, device_id_type=MESH)

    cot_loads = []
    piece = COLUMNS // PARTS
    for q in range(PARTS):
        copy = pltpu.make_async_copy(
            cot_hbm.at[:, pl.ds(q * piece, piece)], cot.at[:, pl.ds(q * piece, piece)], cot_sem.at[q]
        )
        copy.start()
        cot_loads.append(copy)
    chan_load = load(open_hbm, chan, 3)
    thaw_load = load(thaw_hbm, thaw, 4)
    slide_load = load(slide_hbm, slide, 5)
    fric_load = load(fric_hbm, fric, 6)
    map_load = load(map_hbm, cmap, 7)

    lane = lax.broadcasted_iota(jnp.int32, (1, LANES), 1)
    edge_rows = jnp.zeros((4 * MSG, LANES), jnp.float32)
    for ref in (recv1, recv2):
        ref[0 : 4 * MSG, :] = edge_rows
        ref[(TALL - 4) * MSG : TALL * MSG, :] = edge_rows

    owner_load.wait()
    owners = owner[...]
    starts = [jnp.int32(0)]
    for t in range(1, TILES):
        below = jnp.where(owners < t, 1.0, 0.0).astype(jnp.float32)
        partial = jnp.sum(below.reshape(ROWS // 8, 8, LANES), axis=0)
        starts.append(jnp.clip(jnp.sum(partial).astype(jnp.int32), 0, COLUMNS))
    starts.append(jnp.int32(COLUMNS))
    for t in range(TILES + 1):
        begins[t] = starts[t]

    slot = lax.broadcasted_iota(jnp.int32, (MSG, LANES), 0) * LANES + lax.broadcasted_iota(
        jnp.int32, (MSG, LANES), 1
    )

    def window(ref, begin, end):
        first = lax.shift_right_logical(begin, 7)
        turn = lax.bitwise_and(begin, LANES - 1)
        back_turn = lax.bitwise_and(LANES - turn, LANES - 1)
        low = pltpu.roll(ref[pl.ds(first, MSG), :], back_turn, 1)
        high = pltpu.roll(ref[pl.ds(first + 1, MSG), :], back_turn, 1)
        both = jnp.where(lane < LANES - turn, low, high)
        return jnp.where(slot < end - begin, both, 0.0)

    def post(src, dst, number, where):
        copy = pltpu.make_async_remote_copy(
            src_ref=src, dst_ref=dst, send_sem=send_sem.at[number], recv_sem=recv_sem.at[number],
            device_id=where, device_id_type=MESH,
        )
        copy.start()
        return copy

    def keep_own(src, dst, self_number):
        own = pltpu.make_async_copy(
            src.at[rows_at(a * MSG, MSG)], dst.at[rows_at((EDGE + a) * MSG, MSG)], self_sem.at[self_number]
        )
        own.start()
        return own

    def outward(far, order):
        return far + (1 - 2 * (order % 2)) * ((order + 1) // 2)

    def far_first(order):
        away_z = outward(RING_Z // 2, order // RING_Y)
        away_y = outward(RING_Y // 2, order % RING_Y)
        return lax.rem(a // RING_Z + away_y, RING_Y) * RING_Z + lax.rem(a + away_z, RING_Z)

    def to_all(src, dst, number, self_number):
        def one(order, carry):
            target = far_first(order)
            post(src.at[rows_at(target * MSG, MSG)], dst.at[rows_at((EDGE + a) * MSG, MSG)], number, {"col": target})
            return carry

        lax.fori_loop(0, TILES - 1, one, 0)
        return keep_own(src, dst, self_number)

    def all_done(buffer, rows, sem):
        pltpu.make_async_copy(buffer.at[pl.ds(0, rows)], buffer.at[pl.ds(0, rows)], sem).wait()

    store_load.wait()
    melt_load.wait()
    for group in range(TILES // 8):
        targets = [far_first(order) for order in range(group * 8, (group + 1) * 8)]
        for t in targets:
            at = pl.multiple_of(t * MSG, MSG)
            begin, end = begins[t], begins[t + 1]
            stored = window(store, begin, end)
            melted = window(melt, begin, end)
            send1[pl.ds(at, RUN), :] = stored[:RUN]
            send1[pl.ds(at + RUN, MSG - RUN), :] = melted[: MSG - RUN]
            send2[pl.ds(at, 2 * RUN - MSG), :] = melted[MSG - RUN : RUN]
        if group == 0:
            pl.semaphore_wait(barrier, TILES - 1 + 2 + 2)
        for t in targets[: TILES - 1 - group * 8]:
            post(send1.at[rows_at(t * MSG, MSG)], recv1.at[rows_at((EDGE + a) * MSG, MSG)], 2, {"col": t})
    own1 = keep_own(send1, recv1, 0)
    chan_load.wait()
    cond[EDGE : EDGE + TILES, : RUN * LANES] = jnp.where(chan[...] == 1, diffusion_rate, 0.25 * diffusion_rate)
    chan_low = post(cond.at[EDGE : EDGE + TILES, (RUN - 1) * LANES : RUN * LANES], cond_low, 0, {"col": right})
    chan_high = post(cond.at[EDGE : EDGE + TILES, 0:LANES], cond_high, 1, {"col": left})

    weight = jnp.broadcast_to(inverse_ref[:, LAYERS - 1 : LAYERS], (LAYERS, LANES))
    sublane = lax.broadcasted_iota(jnp.int32, (8, LANES), 0)
    thaw_load.wait()
    slide_load.wait()
    fric_load.wait()
    for q in range(PARTS):
        cot_loads[q].wait()

        def last_layer(j, carry):
            block = jnp.zeros((8, LANES), jnp.float32)
            for k in range(8):
                layers = cot[:, pl.ds(pl.multiple_of(j * 1024 + k * LANES, LANES), LANES)]
                total = jnp.sum(layers * weight, axis=0, keepdims=True)
                block = jnp.where(sublane == k, total, block)
            at = rows_at(j * 8, 8)
            base = thaw[at, :].astype(jnp.float32) * slide[at, :] * block
            basal[at, :] = base
            source[at, :] = fric[at, :] * base
            return carry

        lax.fori_loop(q * 8, (q + 1) * 8, last_layer, 0)

    for t in range(TILES):
        send2[MSG * t + 2 * RUN - MSG : MSG * t + 3 * RUN - MSG, :] = window(source, starts[t], starts[t + 1])[:RUN]

    tile = lax.broadcasted_iota(jnp.int32, (TILES, LANES), 0)
    lanes = lax.broadcasted_iota(jnp.int32, (TILES, LANES), 1)

    def beside(first, last):
        ahead = jnp.where(tile == TILES - 1, 0.0, pltpu.roll(first, TILES - 1, 0))
        behind = jnp.where(tile == 0, 0.0, pltpu.roll(last, 1, 0))
        return jnp.where(lanes < 4, ahead, jnp.where(lanes >= LANES - 4, behind, 0.0))

    def every(ref, row):
        return ref[pl.ds(row, TILES, stride=MSG), :]

    send2[pl.ds(14, TILES, stride=MSG), :] = beside(every(send2, 4), every(send2, 13))
    melt_sides = beside(every(send1, 10), every(send2, 3))
    store_sides = beside(every(send1, 0), every(send1, 9))
    store_moved = jnp.where(
        lanes < 64, pltpu.roll(store_sides, 4, 1), pltpu.roll(store_sides, LANES - 4, 1)
    )
    send2[pl.ds(15, TILES, stride=MSG), :] = jnp.where(
        jnp.logical_or(lanes < 4, lanes >= LANES - 4), melt_sides, store_moved
    )
    own2 = to_all(send2, recv2, 3, 1)

    tall = 8 * LAYER_ROWS
    half = jnp.bfloat16
    dot = functools.partial(jnp.dot, preferred_element_type=jnp.float32)
    layer = lax.rem(lax.broadcasted_iota(jnp.int32, (tall, LAYERS), 0), LAYER_ROWS)
    spread = (layer == lax.broadcasted_iota(jnp.int32, (tall, LAYERS), 1)).astype(jnp.float32).astype(half)
    block = lax.broadcasted_iota(jnp.int32, (tall, tall), 0) // LAYER_ROWS
    own_block = block == lax.broadcasted_iota(jnp.int32, (tall, tall), 1) // LAYER_ROWS

    def diagonal(part):
        rows = dot(spread, part).astype(half)
        full = lax.dot_general(rows, spread, (((1,), (1,)), ((), ())), preferred_element_type=jnp.float32)
        return jnp.where(own_block, full, 0.0).astype(half)

    matrix = inverse_ref[...].T
    matrix_high = matrix.astype(half)
    high = diagonal(matrix_high)
    low = diagonal((matrix - matrix_high.astype(jnp.float32)).astype(half))
    pad = jnp.zeros((LAYER_ROWS - LAYERS, 2 * LANES), jnp.float32)
    step = 16 * LANES

    def product_of(n, carry):
        def columns_of(k):
            return pl.ds(pl.multiple_of(n * step + 2 * k * LANES, 2 * LANES), 2 * LANES)

        tiles = []
        for k in range(8):
            tiles += [cot[:, columns_of(k)], pad]
        values = jnp.concatenate(tiles, axis=0)
        values_high = values.astype(half)
        values_low = (values - values_high.astype(jnp.float32)).astype(half)
        result = dot(high, values_high) + (dot(high, values_low) + dot(low, values_high))
        for k in range(8):
            adj[:, columns_of(k)] = result[k * LAYER_ROWS : k * LAYER_ROWS + LAYERS]
        return carry

    lax.fori_loop(0, COLUMNS // step, product_of, 0)
    adj_copy = pltpu.make_async_copy(adj, adj_hbm, out_sem.at[2])
    adj_copy.start()

    chan_low.wait_recv()
    chan_high.wait_recv()
    low_side = jnp.where(jnp.logical_and(lanes >= LANES - 4, a > 0), cond_low[...], 0.0)
    cond[EDGE : EDGE + TILES, RUN * LANES :] = jnp.where(
        jnp.logical_and(lanes < 4, a < TILES - 1), cond_high[...], low_side
    )
    chan_up = post(cond.at[pl.ds(EDGE, EDGE)], cond.at[pl.ds(EDGE + TILES, EDGE)], 4, {"grp": up})
    chan_down = post(cond.at[pl.ds(TILES, EDGE)], cond.at[pl.ds(0, EDGE)], 5, {"grp": down})

    def rows_beside(buffer, number):
        first = post(
            buffer.at[pl.ds(EDGE * MSG, 4 * MSG)], buffer.at[pl.ds((EDGE + TILES) * MSG, 4 * MSG)], number, {"grp": up}
        )
        second = post(
            buffer.at[pl.ds((TILES + 4) * MSG, 4 * MSG)], buffer.at[pl.ds(4 * MSG, 4 * MSG)], number + 1, {"grp": down}
        )
        return first, second

    others = (TILES - 1) * MSG
    own1.wait()
    all_done(recv1, others, recv_sem.at[2])
    rows1 = rows_beside(recv1, 6)
    chan_up.wait_recv()
    chan_down.wait_recv()
    for copy in rows1:
        copy.wait_recv()

    row = lax.broadcasted_iota(jnp.int32, (TALL, LANES), 0)
    inside = jnp.logical_and(
        jnp.logical_or(row >= EDGE, g > 0), jnp.logical_or(row < EDGE + TILES, g < GROUP - 1)
    )

    def mesh_rows(ref, k):
        return ref[pl.ds(k, TALL, stride=MSG), :]

    for k in range(RUN):
        at = slice(k * LANES, (k + 1) * LANES)
        coef[:, at] = jnp.where(inside, cond[:, at] / (1.0 + mesh_rows(recv1, k)), 0.0)

    own2.wait()
    all_done(recv2, others, recv_sem.at[3])
    rows2 = rows_beside(recv2, 8)
    for copy in rows2:
        copy.wait_recv()

    side = mesh_rows(recv2, 15)
    lane_tall = lax.broadcasted_iota(jnp.int32, (TALL, LANES), 1)
    store_side = jnp.where(lane_tall < 64, pltpu.roll(side, LANES - 4, 1), pltpu.roll(side, 4, 1))
    used = jnp.logical_or(lane_tall < 4, lane_tall >= LANES - 4)
    store_side = jnp.where(used, store_side, 0.0)
    melt_side = jnp.where(used, side, 0.0)
    at = slice(RUN * LANES, WIDE)
    coef[:, at] = jnp.where(inside, cond[:, at] / (1.0 + store_side), 0.0)
    melts = [mesh_rows(recv1, RUN + k) for k in range(MSG - RUN)]
    melts += [mesh_rows(recv2, k) for k in range(2 * RUN - MSG)] + [melt_side]
    keeps = [1.0 - melt_rate * part for part in melts]
    now = [jnp.where(inside, mesh_rows(recv2, 2 * RUN - MSG + k), 0.0) for k in range(RUN + 1)]
    keep = jnp.concatenate(keeps, axis=1)
    field = jnp.concatenate(now, axis=1)
    pressure[...] = field
    for sweep in range(HSWEEPS):
        field = pressure[...]
        rate = coef[...]
        sides = (
            pltpu.roll(field, 1, 1) + pltpu.roll(field, WIDE - 1, 1) + pltpu.roll(field, 1, 0) + pltpu.roll(field, TALL - 1, 0)
        )
        pressure[...] = keep * field + rate * (sides - 4.0 * field)

    for k in range(RUN):
        for i in range(TILES // 8):
            cells = pressure[EDGE + 8 * i : EDGE + 8 * i + 8, k * LANES : (k + 1) * LANES]
            back_send[pl.ds(8 * i * MSG + k, 8, stride=MSG), :] = cells
    press_out[...] = pressure[EDGE : EDGE + TILES, : RUN * LANES]
    press_copy = pltpu.make_async_copy(press_out, press_hbm, out_sem.at[0])
    press_copy.start()

    pad0 = LEVELS[0][1]

    for order in range(TILES - 1):
        target = far_first(order)
        post(
            back_send.at[rows_at(target * MSG, RUN)], lev0.at[a, pl.ds(pad0, RUN)], 10, {"col": target}
        )
    own_back = pltpu.make_async_copy(
        back_send.at[rows_at(a * MSG, RUN)], lev0.at[a, pl.ds(pad0, RUN)], self_sem.at[2]
    )
    own_back.start()
    own_back.wait()
    all_done(back_send, (TILES - 1) * RUN, recv_sem.at[10])

    levels = (lev0, lev1, lev2, lev3, lev4)
    for level, (nodes, pad, tall) in enumerate(LEVELS):
        ref = levels[level]
        index = lax.broadcasted_iota(jnp.int32, (tall, LANES), 0) * LANES + lax.broadcasted_iota(
            jnp.int32, (tall, LANES), 1
        )
        for node in range(nodes // 2):
            begin = starts[(2 * node) << level]
            length = jnp.clip(starts[(2 * node + 1) << level] - begin, 0, (RUN << level) * LANES)
            first = lax.shift_right_logical(length, 7)
            turn = lax.bitwise_and(length, LANES - 1)
            mine_rows = ref[2 * node, pl.ds(pad, tall), :]
            here = pltpu.roll(ref[2 * node + 1, pl.ds(pad - first, tall), :], turn, 1)
            before = pltpu.roll(ref[2 * node + 1, pl.ds(pad - 1 - first, tall), :], turn, 1)
            moved = jnp.where(lane >= turn, here, before)
            merged = jnp.where(index < length, mine_rows, moved)
            if level < len(LEVELS) - 1:
                levels[level + 1][node, pl.ds(LEVELS[level + 1][1], tall), :] = merged
            else:
                value = thaw[...].astype(jnp.float32) * fric[...] * (basal[...] + merged)
                sens[...] = value

    sens_copy = pltpu.make_async_copy(sens, sens_hbm, out_sem.at[1])
    sens_copy.start()

    def pass_on(q, slot, src, ahead):
        copy = pltpu.make_async_remote_copy(
            src_ref=src.at[pl.ds(q * PART, PART)],
            dst_ref=gathered.at[slot, pl.ds(q * PART, PART)],
            send_sem=part_send.at[q, slot - 1],
            recv_sem=part_recv.at[q, slot - 1],
            device_id={"grp": lax.rem(chip + ahead, CHIPS) * 2 + core},
            device_id_type=MESH,
        )
        copy.start()
        return copy

    parts = {}
    for q in range(PARTS):
        parts[q, 1] = pass_on(q, 1, sens, 1)
        other = (q + PARTS // 2) % PARTS
        parts[other, 3] = pass_on(other, 3, sens, CHIPS - 1)
    in_order = []
    for q in range(PARTS // 2):
        other = q + PARTS // 2
        parts[q, 1].wait_recv()
        parts[q, 2] = pass_on(q, 2, gathered.at[1], 1)
        parts[other, 3].wait_recv()
        parts[other, 2] = pass_on(other, 2, gathered.at[3], CHIPS - 1)
        in_order += [q, other]

    def factor(who, d):
        return mix_ref[who, lax.rem(chip + CHIPS - d, CHIPS) * 2 + core]

    to_self = [factor(g, d) for d in range(CHIPS)]
    to_other = [factor(sibling, d) for d in range(CHIPS)]
    pairs = {}
    for q in in_order:
        at = pl.ds(q * PART, PART)
        parts[q, 3 if q < PARTS // 2 else 1].wait_recv()
        parts[q, 2].wait_recv()
        pieces = [sens[at, :]] + [gathered[d, at, :] for d in range(1, CHIPS)]
        other_send[at, :] = sum(to_other[d] * pieces[d] for d in range(CHIPS))
        copy = pltpu.make_async_remote_copy(
            src_ref=other_send.at[at], dst_ref=other_recv.at[at], send_sem=pair_send.at[q], recv_sem=pair_recv.at[q],
            device_id={"grp": sibling}, device_id_type=MESH,
        )
        copy.start()
        pairs[q] = copy
        mine[at, :] = sum(to_self[d] * pieces[d] for d in range(CHIPS))

    map_load.wait()
    total = jnp.zeros((CONTROLS, LANES), jnp.float32)
    for q in in_order:
        pairs[q].wait_recv()

        def product(j, total):
            at = rows_at(j * 8, 8)
            mixed = (mine[at, :] + other_recv[at, :]).astype(jnp.bfloat16).astype(jnp.float32)
            for s in range(8):
                block = cmap[:, pl.ds(pl.multiple_of(j * 1024 + s * LANES, LANES), LANES)]
                total = total + block.astype(jnp.float32) * mixed[s : s + 1, :]
            return total

        total = lax.fori_loop(q * PART // 8, (q + 1) * PART // 8, product, total)
    grad_ref[...] = jnp.sum(total.T, axis=0, keepdims=True)

    chan_low.wait_send()
    chan_high.wait_send()
    chan_up.wait_send()
    chan_down.wait_send()
    for copy in rows1 + rows2:
        copy.wait_send()
    all_done(send1, others, send_sem.at[2])
    all_done(send2, others, send_sem.at[3])
    all_done(back_send, (TILES - 1) * RUN, send_sem.at[10])
    for copy in list(parts.values()) + list(pairs.values()):
        copy.wait_send()
    press_copy.wait()
    sens_copy.wait()
    adj_copy.wait()


def hand_on_kernel(
    adj_in, press_in, sens_in, grad_in, adj_out, press_out, sens_out, grad_out, adj, press, sens, grad, in_sem, out_sem
):
    width = COLUMNS // PIECES
    moves = [(press_in, press, press_out), (sens_in, sens, sens_out), (grad_in, grad, grad_out)]
    for q in range(PIECES):
        at = pl.ds(q * width, width)
        moves.append((adj_in.at[:, at], adj.at[:, at], adj_out.at[:, at]))
    ins, outs = [], []
    for number, (src, held, dst) in enumerate(moves):
        ins.append(pltpu.make_async_copy(src, held, in_sem.at[number]))
        outs.append(pltpu.make_async_copy(held, dst, out_sem.at[number]))
        ins[-1].start()
    for came, goes in zip(ins, outs):
        came.wait()
        goes.start()
    for goes in outs:
        goes.wait()

def on_device(
    velocity_cotangent,
    vertical_inverse,
    sliding_speed,
    friction_coef,
    thawed_bed,
    basal_melt,
    storage_coef,
    owner_tile,
    channel_open,
    group_mix,
    control_map,
):
    shaped = [x.reshape(ROWS, LANES) for x in (sliding_speed, friction_coef, thawed_bed, basal_melt, storage_coef, owner_tile)]
    f32 = jnp.float32
    anywhere = pl.BlockSpec(memory_space=pltpu.HBM)
    vmem = pl.BlockSpec(memory_space=pltpu.VMEM)
    columns = pltpu.VMEM((ROWS, LANES), f32)
    padded = pltpu.VMEM((ROWS + 24, LANES), f32)
    numbers = pltpu.VMEM((ROWS, LANES), jnp.int32)
    messages = pltpu.VMEM(((TILES + 1) * MSG, LANES), f32)
    received = pltpu.VMEM(((TALL + 1) * MSG, LANES), f32)
    field = pltpu.VMEM((TALL, WIDE), f32)
    dma = pltpu.SemaphoreType.DMA
    results = pl.pallas_call(
        kernel,
        out_shape=(
            jax.ShapeDtypeStruct((LAYERS, COLUMNS), f32),
            jax.ShapeDtypeStruct((TILES, RUN * LANES), f32),
            jax.ShapeDtypeStruct((ROWS, LANES), f32),
            jax.ShapeDtypeStruct((1, CONTROLS), f32),
        ),
        in_specs=[pl.BlockSpec(memory_space=pltpu.SMEM), vmem] + [anywhere] * 9,
        out_specs=(anywhere, anywhere, anywhere, vmem),
        scratch_shapes=[
            pltpu.VMEM((LAYERS, COLUMNS), f32), pltpu.VMEM((LAYERS, COLUMNS), f32),
            pltpu.VMEM((CONTROLS, COLUMNS), jnp.bfloat16),
            columns, columns, numbers, padded, padded, numbers,
            pltpu.VMEM((TILES, RUN * LANES), jnp.int32),
            padded, columns,
            messages, messages, received, received,
            field, pltpu.VMEM((TILES, LANES), f32), pltpu.VMEM((TILES, LANES), f32),
            field, field, pltpu.VMEM((TILES, RUN * LANES), f32), messages,
        ]
        + [pltpu.VMEM((nodes, pad + tall, LANES), f32) for nodes, pad, tall in LEVELS]
        + [
            columns, pltpu.VMEM((CHIPS, ROWS, LANES), f32), columns, columns, columns,
            pltpu.SMEM((TILES + 1,), jnp.int32), dma((8,)), dma((PARTS,)), dma((3,)), dma((11,)), dma((11,)),
            dma((PARTS, CHIPS - 1)), dma((PARTS, CHIPS - 1)), dma((PARTS,)), dma((PARTS,)), dma((3,)),
        ],
        compiler_params=pltpu.CompilerParams(
            collective_id=0, has_side_effects=True, vmem_limit_bytes=VMEM_BYTES
        ),
    )(group_mix, vertical_inverse, velocity_cotangent, *shaped, channel_open, control_map)
    adjoint, pressure, sensitivity, gradient = pl.pallas_call(
        hand_on_kernel,
        out_shape=tuple(jax.ShapeDtypeStruct(x.shape, x.dtype) for x in results),
        in_specs=[anywhere] * 4,
        out_specs=(anywhere,) * 4,
        scratch_shapes=[pltpu.VMEM(x.shape, x.dtype) for x in results] + [dma((3 + PIECES,)), dma((3 + PIECES,))],
        compiler_params=pltpu.CompilerParams(vmem_limit_bytes=VMEM_BYTES),
    )(*results)
    return adjoint, pressure, sensitivity.reshape(COLUMNS), gradient.reshape(CONTROLS)


def solution(mesh):
    in_specs = (
        P(None, ("col", "grp")),
        P(),
        P(("col", "grp")),
        P(("col", "grp")),
        P(("col", "grp")),
        P(("col", "grp")),
        P(("col", "grp")),
        P(("col", "grp"), None),
        P("grp", "col"),
        P(),
        P(("col", "grp"), None),
    )
    out_specs = (P(None, ("col", "grp")), P("grp", "col"), P(("col", "grp")), P(("col", "grp")))
    return jax.shard_map(
        on_device, mesh=mesh, in_specs=in_specs, out_specs=out_specs, check_vma=False
    )
```

```python
import functools

import jax
import jax.numpy as jnp
from jax import lax
from jax.experimental import pallas as pl
from jax.experimental.pallas import tpu as pltpu
from jax.sharding import PartitionSpec as P

HSWEEPS = 4
diffusion_rate = 0.12
melt_rate = 0.3

TILES = 32
GROUP = 8
CHIPS = 4
RING_Y, RING_Z = 4, 8
COLUMNS = 32768
LAYERS = 20
LAYER_ROWS = 24
LANES = 128
ROWS = COLUMNS // LANES
RUN = 10
MSG = 16
EDGE = 8
WIDE = RUN * LANES + LANES
TALL = TILES + 2 * EDGE
CONTROLS = 64
PIECES = 4
PARTS = 4
PART = ROWS // PARTS
PART_ORDER = [q + half for q in range(PARTS // 2) for half in (0, PARTS // 2)]
MESH = pl.DeviceIdType.MESH
VMEM_BYTES = 64 * 1024 * 1024

LEVELS = ((32, 16, 24), (16, 24, 40), (8, 48, 80), (4, 88, 160), (2, 168, 256))


def rows_at(start, count):
    return pl.ds(pl.multiple_of(start, 8), count)


def kernel(
    mix_ref, inverse_ref, cot_hbm, slide_hbm, fric_hbm, thaw_hbm, melt_hbm, store_hbm, owner_hbm, open_hbm, map_hbm,
    adj_hbm, press_hbm, sens_hbm, grad_ref,
    cot, adj, cmap, slide, fric, thaw, melt, store, owner, chan, source, basal,
    send1, send2, recv1, recv2, edge2, cond, cond_low, cond_high, coef, pressure, press_out, back_send,
    lev0, lev1, lev2, lev3, lev4, sens, gathered, other_send, other_recv, mine,
    begins, load_sem, cot_sem, self_sem, send_sem, recv_sem, part_send, part_recv, pair_send, pair_recv, out_sem,
):
    a = lax.axis_index("col")
    g = lax.axis_index("grp")
    chip = g // 2
    core = lax.rem(g, 2)
    sibling = chip * 2 + (1 - core)
    up = lax.rem(g + GROUP - 1, GROUP)
    down = lax.rem(g + 1, GROUP)
    left = lax.rem(a + TILES - 1, TILES)
    right = lax.rem(a + 1, TILES)

    def load(src, dst, number):
        copy = pltpu.make_async_copy(src, dst, load_sem.at[number])
        copy.start()
        return copy

    owner_load = load(owner_hbm, owner, 0)
    melt_load = load(melt_hbm, melt.at[pl.ds(0, ROWS)], 1)
    store_load = load(store_hbm, store.at[pl.ds(0, ROWS)], 2)
    barrier = pltpu.get_barrier_semaphore()

    def greet(d, carry):
        pl.semaphore_signal(
            barrier, inc=1, device_id={"col": lax.rem(a + d, TILES)}, device_id_type=MESH
        )
        return carry

    lax.fori_loop(1, TILES, greet, 0)
    for other in (up, down):
        pl.semaphore_signal(barrier, inc=1, device_id={"grp": other}, device_id_type=MESH)
    for d in (1, CHIPS - 1):
        same_core = lax.rem(chip + d, CHIPS) * 2 + core
        pl.semaphore_signal(barrier, inc=1, device_id={"grp": same_core}, device_id_type=MESH)

    cot_loads = []
    piece = COLUMNS // PARTS
    for q in range(PARTS):
        copy = pltpu.make_async_copy(
            cot_hbm.at[:, pl.ds(q * piece, piece)], cot.at[:, pl.ds(q * piece, piece)], cot_sem.at[q]
        )
        copy.start()
        cot_loads.append(copy)
    chan_load = load(open_hbm, chan, 3)
    thaw_load = load(thaw_hbm, thaw, 4)
    slide_load = load(slide_hbm, slide, 5)
    fric_load = load(fric_hbm, fric, 6)
    map_load = load(map_hbm, cmap, 7)

    lane = lax.broadcasted_iota(jnp.int32, (1, LANES), 1)
    edge_rows = jnp.zeros((4 * MSG, LANES), jnp.float32)
    recv1[0 : 4 * MSG, :] = edge_rows
    recv1[(TALL - 4) * MSG : TALL * MSG, :] = edge_rows
    edge2[0 : 4 * MSG, :] = edge_rows
    edge2[(EDGE + 4) * MSG : 2 * EDGE * MSG, :] = edge_rows

    owner_load.wait()
    owners = owner[...]
    starts = [jnp.int32(0)]
    for t in range(1, TILES):
        below = jnp.where(owners < t, 1.0, 0.0).astype(jnp.float32)
        partial = jnp.sum(below.reshape(ROWS // 8, 8, LANES), axis=0)
        starts.append(jnp.clip(jnp.sum(partial).astype(jnp.int32), 0, COLUMNS))
    starts.append(jnp.int32(COLUMNS))
    for t in range(TILES + 1):
        begins[t] = starts[t]

    slot = lax.broadcasted_iota(jnp.int32, (MSG, LANES), 0) * LANES + lax.broadcasted_iota(
        jnp.int32, (MSG, LANES), 1
    )

    def window(ref, begin, end):
        first = lax.shift_right_logical(begin, 7)
        turn = lax.bitwise_and(begin, LANES - 1)
        back_turn = lax.bitwise_and(LANES - turn, LANES - 1)
        low = pltpu.roll(ref[pl.ds(first, MSG), :], back_turn, 1)
        high = pltpu.roll(ref[pl.ds(first + 1, MSG), :], back_turn, 1)
        both = jnp.where(lane < LANES - turn, low, high)
        return jnp.where(slot < end - begin, both, 0.0)

    def post(src, dst, number, where):
        copy = pltpu.make_async_remote_copy(
            src_ref=src, dst_ref=dst, send_sem=send_sem.at[number], recv_sem=recv_sem.at[number],
            device_id=where, device_id_type=MESH,
        )
        copy.start()
        return copy

    def keep_own(src, dst, self_number):
        own = pltpu.make_async_copy(
            src.at[rows_at(a * MSG, MSG)], dst.at[rows_at((EDGE + a) * MSG, MSG)], self_sem.at[self_number]
        )
        own.start()
        return own

    def outward(far, order):
        return far + (1 - 2 * (order % 2)) * ((order + 1) // 2)

    def far_first(order):
        away_z = outward(RING_Z // 2, order // RING_Y)
        away_y = outward(RING_Y // 2, order % RING_Y)
        return lax.rem(a // RING_Z + away_y, RING_Y) * RING_Z + lax.rem(a + away_z, RING_Z)

    def to_all(src, dst, number, self_number):
        def one(order, carry):
            target = far_first(order)
            post(src.at[rows_at(target * MSG, MSG)], dst.at[rows_at((EDGE + a) * MSG, MSG)], number, {"col": target})
            return carry

        lax.fori_loop(0, TILES - 1, one, 0)
        return keep_own(src, dst, self_number)

    def all_done(buffer, rows, sem):
        pltpu.make_async_copy(buffer.at[pl.ds(0, rows)], buffer.at[pl.ds(0, rows)], sem).wait()

    store_load.wait()
    melt_load.wait()
    for group in range(TILES // 8):
        targets = [far_first(order) for order in range(group * 8, (group + 1) * 8)]
        for t in targets:
            at = pl.multiple_of(t * MSG, MSG)
            begin, end = begins[t], begins[t + 1]
            stored = window(store, begin, end)
            melted = window(melt, begin, end)
            send1[pl.ds(at, RUN), :] = stored[:RUN]
            send1[pl.ds(at + RUN, MSG - RUN), :] = melted[: MSG - RUN]
            send2[pl.ds(at, 2 * RUN - MSG), :] = melted[MSG - RUN : RUN]
        if group == 0:
            pl.semaphore_wait(barrier, TILES - 1 + 2 + 2)
        for t in targets[: TILES - 1 - group * 8]:
            post(send1.at[rows_at(t * MSG, MSG)], recv1.at[rows_at((EDGE + a) * MSG, MSG)], 2, {"col": t})
    own1 = keep_own(send1, recv1, 0)
    chan_load.wait()
    cond[EDGE : EDGE + TILES, : RUN * LANES] = jnp.where(chan[...] == 1, diffusion_rate, 0.25 * diffusion_rate)
    chan_low = post(cond.at[EDGE : EDGE + TILES, (RUN - 1) * LANES : RUN * LANES], cond_low, 0, {"col": right})
    chan_high = post(cond.at[EDGE : EDGE + TILES, 0:LANES], cond_high, 1, {"col": left})

    weight = jnp.broadcast_to(inverse_ref[:, LAYERS - 1 : LAYERS], (LAYERS, LANES))
    sublane = lax.broadcasted_iota(jnp.int32, (8, LANES), 0)
    thaw_load.wait()
    slide_load.wait()
    fric_load.wait()
    for q in range(PARTS):
        cot_loads[q].wait()

        def last_layer(j, carry):
            block = jnp.zeros((8, LANES), jnp.float32)
            for k in range(8):
                layers = cot[:, pl.ds(pl.multiple_of(j * 1024 + k * LANES, LANES), LANES)]
                total = jnp.sum(layers * weight, axis=0, keepdims=True)
                block = jnp.where(sublane == k, total, block)
            at = rows_at(j * 8, 8)
            base = thaw[at, :].astype(jnp.float32) * slide[at, :] * block
            basal[at, :] = base
            source[at, :] = fric[at, :] * base
            return carry

        lax.fori_loop(q * 8, (q + 1) * 8, last_layer, 0)

    for t in range(TILES):
        send2[MSG * t + 2 * RUN - MSG : MSG * t + 3 * RUN - MSG, :] = window(source, starts[t], starts[t + 1])[:RUN]

    tile = lax.broadcasted_iota(jnp.int32, (TILES, LANES), 0)
    lanes = lax.broadcasted_iota(jnp.int32, (TILES, LANES), 1)

    def beside(first, last):
        ahead = jnp.where(tile == TILES - 1, 0.0, pltpu.roll(first, TILES - 1, 0))
        behind = jnp.where(tile == 0, 0.0, pltpu.roll(last, 1, 0))
        return jnp.where(lanes < 4, ahead, jnp.where(lanes >= LANES - 4, behind, 0.0))

    def every(ref, row):
        return ref[pl.ds(row, TILES, stride=MSG), :]

    send2[pl.ds(14, TILES, stride=MSG), :] = beside(every(send2, 4), every(send2, 13))
    melt_sides = beside(every(send1, 10), every(send2, 3))
    store_sides = beside(every(send1, 0), every(send1, 9))
    store_moved = jnp.where(
        lanes < 64, pltpu.roll(store_sides, 4, 1), pltpu.roll(store_sides, LANES - 4, 1)
    )
    send2[pl.ds(15, TILES, stride=MSG), :] = jnp.where(
        jnp.logical_or(lanes < 4, lanes >= LANES - 4), melt_sides, store_moved
    )
    own2 = to_all(send2, recv2, 3, 1)

    tall = 8 * LAYER_ROWS
    half = jnp.bfloat16
    dot = functools.partial(jnp.dot, preferred_element_type=jnp.float32)
    layer = lax.rem(lax.broadcasted_iota(jnp.int32, (tall, LAYERS), 0), LAYER_ROWS)
    spread = (layer == lax.broadcasted_iota(jnp.int32, (tall, LAYERS), 1)).astype(jnp.float32).astype(half)
    block = lax.broadcasted_iota(jnp.int32, (tall, tall), 0) // LAYER_ROWS
    own_block = block == lax.broadcasted_iota(jnp.int32, (tall, tall), 1) // LAYER_ROWS

    def diagonal(part):
        rows = dot(spread, part).astype(half)
        full = lax.dot_general(rows, spread, (((1,), (1,)), ((), ())), preferred_element_type=jnp.float32)
        return jnp.where(own_block, full, 0.0).astype(half)

    matrix = inverse_ref[...].T
    matrix_high = matrix.astype(half)
    high = diagonal(matrix_high)
    low = diagonal((matrix - matrix_high.astype(jnp.float32)).astype(half))
    pad = jnp.zeros((LAYER_ROWS - LAYERS, 2 * LANES), jnp.float32)
    step = 16 * LANES

    def product_of(n, carry):
        def columns_of(k):
            return pl.ds(pl.multiple_of(n * step + 2 * k * LANES, 2 * LANES), 2 * LANES)

        tiles = []
        for k in range(8):
            tiles += [cot[:, columns_of(k)], pad]
        values = jnp.concatenate(tiles, axis=0)
        values_high = values.astype(half)
        values_low = (values - values_high.astype(jnp.float32)).astype(half)
        result = dot(high, values_high) + (dot(high, values_low) + dot(low, values_high))
        for k in range(8):
            adj[:, columns_of(k)] = result[k * LAYER_ROWS : k * LAYER_ROWS + LAYERS]
        return carry

    lax.fori_loop(0, COLUMNS // step, product_of, 0)
    adj_copy = pltpu.make_async_copy(adj, adj_hbm, out_sem.at[2])
    adj_copy.start()

    chan_low.wait_recv()
    chan_high.wait_recv()
    low_side = jnp.where(jnp.logical_and(lanes >= LANES - 4, a > 0), cond_low[...], 0.0)
    cond[EDGE : EDGE + TILES, RUN * LANES :] = jnp.where(
        jnp.logical_and(lanes < 4, a < TILES - 1), cond_high[...], low_side
    )
    chan_up = post(cond.at[pl.ds(EDGE, EDGE)], cond.at[pl.ds(EDGE + TILES, EDGE)], 4, {"grp": up})
    chan_down = post(cond.at[pl.ds(TILES, EDGE)], cond.at[pl.ds(0, EDGE)], 5, {"grp": down})

    def rows_beside(buffer, into, below, number):
        first = post(buffer.at[pl.ds(EDGE * MSG, 4 * MSG)], into.at[pl.ds(below, 4 * MSG)], number, {"grp": up})
        second = post(
            buffer.at[pl.ds((TILES + 4) * MSG, 4 * MSG)], into.at[pl.ds(4 * MSG, 4 * MSG)], number + 1, {"grp": down}
        )
        return first, second

    others = (TILES - 1) * MSG
    own1.wait()
    all_done(recv1, others, recv_sem.at[2])
    rows1 = rows_beside(recv1, recv1, (EDGE + TILES) * MSG, 6)
    chan_up.wait_recv()
    chan_down.wait_recv()
    for copy in rows1:
        copy.wait_recv()

    row = lax.broadcasted_iota(jnp.int32, (TALL, LANES), 0)
    inside = jnp.logical_and(
        jnp.logical_or(row >= EDGE, g > 0), jnp.logical_or(row < EDGE + TILES, g < GROUP - 1)
    )

    def mesh_rows(ref, k):
        return ref[pl.ds(k, TALL, stride=MSG), :]

    for k in range(RUN):
        at = slice(k * LANES, (k + 1) * LANES)
        coef[:, at] = jnp.where(inside, cond[:, at] / (1.0 + mesh_rows(recv1, k)), 0.0)

    own2.wait()
    all_done(recv2, others, recv_sem.at[3])
    rows2 = rows_beside(recv2, edge2, EDGE * MSG, 8)

    last = slice(RUN * LANES, WIDE)
    lane_tall = lax.broadcasted_iota(jnp.int32, (TILES, LANES), 1)
    used = jnp.logical_or(lane_tall < 4, lane_tall >= LANES - 4)

    def sweeps(got1, got2, inside, rate_of):
        side = got2(15)
        store_side = jnp.where(lane_tall < 64, pltpu.roll(side, LANES - 4, 1), pltpu.roll(side, 4, 1))
        store_side = jnp.where(used, store_side, 0.0)
        melts = [got1(RUN + k) for k in range(MSG - RUN)]
        melts += [got2(k) for k in range(2 * RUN - MSG)] + [jnp.where(used, side, 0.0)]
        keep = jnp.concatenate([1.0 - melt_rate * part for part in melts], axis=1)
        rate_side = jnp.where(inside, rate_of(cond, last) / (1.0 + store_side), 0.0)
        rate = jnp.concatenate([rate_of(coef, slice(0, RUN * LANES)), rate_side], axis=1)
        pressure[...] = jnp.concatenate(
            [jnp.where(inside, got2(2 * RUN - MSG + k), 0.0) for k in range(RUN + 1)], axis=1
        )
        for sweep in range(HSWEEPS):
            field = pressure[...]
            sides = (
                pltpu.roll(field, 1, 1)
                + pltpu.roll(field, WIDE - 1, 1)
                + pltpu.roll(field, 1, 0)
                + pltpu.roll(field, TILES - 1, 0)
            )
            pressure[...] = keep * field + rate * (sides - 4.0 * field)

    def own_rows(ref):
        return lambda k: ref[pl.ds(EDGE * MSG + k, TILES, stride=MSG), :]

    pad0 = LEVELS[0][1]

    def give_back(interior):
        def one(order, carry):
            target = far_first(order)
            middle = jnp.logical_and(target >= 4, target < TILES - 4)

            @pl.when(middle if interior else jnp.logical_not(middle))
            def _():
                post(
                    back_send.at[rows_at(target * MSG, RUN)], lev0.at[a, pl.ds(pad0, RUN)], 10, {"col": target}
                )

            return carry

        lax.fori_loop(0, TILES - 1, one, 0)

    sweeps(own_rows(recv1), own_rows(recv2), True, lambda ref, at: ref[EDGE : EDGE + TILES, at])
    for k in range(RUN):
        at = slice(k * LANES, (k + 1) * LANES)
        for i in range(TILES // 8):
            back_send[pl.ds(8 * i * MSG + k, 8, stride=MSG), :] = pressure[8 * i : 8 * i + 8, at]
    press_out[...] = pressure[:, : RUN * LANES]
    give_back(True)

    for copy in rows2:
        copy.wait_recv()

    def band(ref, k):
        return [ref[pl.ds(row * MSG + k, EDGE, stride=MSG), :] for row in (EDGE, TILES)]

    def edge_rows1(k):
        outer = [recv1[pl.ds(row * MSG + k, EDGE, stride=MSG), :] for row in (0, EDGE + TILES)]
        inner = band(recv1, k)
        return jnp.concatenate([outer[0], inner[0], inner[1], outer[1]], axis=0)

    def edge_rows2(k):
        outer = [edge2[pl.ds(row * MSG + k, EDGE, stride=MSG), :] for row in (0, EDGE)]
        inner = band(recv2, k)
        return jnp.concatenate([outer[0], inner[0], inner[1], outer[1]], axis=0)

    band_row = lax.broadcasted_iota(jnp.int32, (TILES, LANES), 0)
    band_inside = jnp.logical_and(
        jnp.logical_or(band_row >= EDGE, g > 0), jnp.logical_or(band_row < TILES - EDGE, g < GROUP - 1)
    )
    sweeps(
        edge_rows1, edge_rows2, band_inside,
        lambda ref, at: jnp.concatenate([ref[0 : 2 * EDGE, at], ref[TILES:TALL, at]], axis=0),
    )
    for k in range(RUN):
        at = slice(k * LANES, (k + 1) * LANES)
        back_send[pl.ds(k, 4, stride=MSG), :] = pressure[EDGE : EDGE + 4, at]
        back_send[pl.ds((TILES - 4) * MSG + k, 4, stride=MSG), :] = pressure[2 * EDGE + 4 : 3 * EDGE, at]
    give_back(False)
    press_out[0:4, :] = pressure[EDGE : EDGE + 4, : RUN * LANES]
    press_out[TILES - 4 : TILES, :] = pressure[2 * EDGE + 4 : 3 * EDGE, : RUN * LANES]
    press_copy = pltpu.make_async_copy(press_out, press_hbm, out_sem.at[0])
    press_copy.start()
    own_back = pltpu.make_async_copy(
        back_send.at[rows_at(a * MSG, RUN)], lev0.at[a, pl.ds(pad0, RUN)], self_sem.at[2]
    )
    own_back.start()
    own_back.wait()
    all_done(back_send, (TILES - 1) * RUN, recv_sem.at[10])

    def pass_on(q, slot, src, ahead):
        copy = pltpu.make_async_remote_copy(
            src_ref=src.at[pl.ds(q * PART, PART)],
            dst_ref=gathered.at[slot, pl.ds(q * PART, PART)],
            send_sem=part_send.at[q, slot - 1],
            recv_sem=part_recv.at[q, slot - 1],
            device_id={"grp": lax.rem(chip + ahead, CHIPS) * 2 + core},
            device_id_type=MESH,
        )
        copy.start()
        return copy

    parts = {}

    def merge(ref, node, pad, length, begin, rows):
        first = lax.shift_right_logical(length, 7)
        turn = lax.bitwise_and(length, LANES - 1)
        index = lax.broadcasted_iota(jnp.int32, (rows, LANES), 0) * LANES + lax.broadcasted_iota(
            jnp.int32, (rows, LANES), 1
        )
        head = ref[2 * node, pl.ds(pad + begin, rows), :]
        here = pltpu.roll(ref[2 * node + 1, pl.ds(pad + begin - first, rows), :], turn, 1)
        before = pltpu.roll(ref[2 * node + 1, pl.ds(pad + begin - 1 - first, rows), :], turn, 1)
        return jnp.where(index < length - begin * LANES, head, jnp.where(lane >= turn, here, before))

    levels = (lev0, lev1, lev2, lev3, lev4)
    for level, (nodes, pad, tall) in enumerate(LEVELS):
        ref = levels[level]
        for node in range(nodes // 2):
            begin = starts[(2 * node) << level]
            length = jnp.clip(starts[(2 * node + 1) << level] - begin, 0, (RUN << level) * LANES)
            for part, rows in ((0, tall),) if level < len(LEVELS) - 1 else tuple((q, PART) for q in PART_ORDER):
                merged = merge(ref, node, pad, length, part * rows, rows)
                if level < len(LEVELS) - 1:
                    levels[level + 1][node, pl.ds(LEVELS[level + 1][1], tall), :] = merged
                else:
                    at = pl.ds(part * PART, PART)
                    sens[at, :] = thaw[at, :].astype(jnp.float32) * fric[at, :] * (basal[at, :] + merged)
                    if part < PARTS // 2:
                        parts[part, 1] = pass_on(part, 1, sens, 1)
                    else:
                        parts[part, 3] = pass_on(part, 3, sens, CHIPS - 1)

    sens_copy = pltpu.make_async_copy(sens, sens_hbm, out_sem.at[1])
    sens_copy.start()

    for q in range(PARTS // 2):
        other = q + PARTS // 2
        parts[other, 1] = pass_on(other, 1, sens, 1)
        parts[q, 3] = pass_on(q, 3, sens, CHIPS - 1)
    in_order = []
    for q in range(PARTS // 2):
        other = q + PARTS // 2
        parts[q, 1].wait_recv()
        parts[q, 2] = pass_on(q, 2, gathered.at[1], 1)
        parts[other, 3].wait_recv()
        parts[other, 2] = pass_on(other, 2, gathered.at[3], CHIPS - 1)
        in_order += [q, other]

    def factor(who, d):
        return mix_ref[who, lax.rem(chip + CHIPS - d, CHIPS) * 2 + core]

    to_self = [factor(g, d) for d in range(CHIPS)]
    to_other = [factor(sibling, d) for d in range(CHIPS)]
    pairs = {}
    for q in in_order:
        at = pl.ds(q * PART, PART)
        parts[q, 3 if q < PARTS // 2 else 1].wait_recv()
        parts[q, 2].wait_recv()
        pieces = [sens[at, :]] + [gathered[d, at, :] for d in range(1, CHIPS)]
        other_send[at, :] = sum(to_other[d] * pieces[d] for d in range(CHIPS))
        copy = pltpu.make_async_remote_copy(
            src_ref=other_send.at[at], dst_ref=other_recv.at[at], send_sem=pair_send.at[q], recv_sem=pair_recv.at[q],
            device_id={"grp": sibling}, device_id_type=MESH,
        )
        copy.start()
        pairs[q] = copy
        mine[at, :] = sum(to_self[d] * pieces[d] for d in range(CHIPS))

    map_load.wait()
    total = jnp.zeros((CONTROLS, LANES), jnp.float32)
    for q in in_order:
        pairs[q].wait_recv()

        def product(j, total):
            at = rows_at(j * 8, 8)
            mixed = (mine[at, :] + other_recv[at, :]).astype(jnp.bfloat16).astype(jnp.float32)
            for s in range(8):
                block = cmap[:, pl.ds(pl.multiple_of(j * 1024 + s * LANES, LANES), LANES)]
                total = total + block.astype(jnp.float32) * mixed[s : s + 1, :]
            return total

        total = lax.fori_loop(q * PART // 8, (q + 1) * PART // 8, product, total)
    grad_ref[...] = jnp.sum(total.T, axis=0, keepdims=True)

    chan_low.wait_send()
    chan_high.wait_send()
    chan_up.wait_send()
    chan_down.wait_send()
    for copy in rows1 + rows2:
        copy.wait_send()
    all_done(send1, others, send_sem.at[2])
    all_done(send2, others, send_sem.at[3])
    all_done(back_send, (TILES - 1) * RUN, send_sem.at[10])
    for copy in list(parts.values()) + list(pairs.values()):
        copy.wait_send()
    press_copy.wait()
    sens_copy.wait()
    adj_copy.wait()


def hand_on_kernel(
    adj_in, press_in, sens_in, grad_in, adj_out, press_out, sens_out, grad_out, adj, press, sens, grad, in_sem, out_sem
):
    width = COLUMNS // PIECES
    moves = [(press_in, press, press_out), (sens_in, sens, sens_out), (grad_in, grad, grad_out)]
    for q in range(PIECES):
        at = pl.ds(q * width, width)
        moves.append((adj_in.at[:, at], adj.at[:, at], adj_out.at[:, at]))
    ins, outs = [], []
    for number, (src, held, dst) in enumerate(moves):
        ins.append(pltpu.make_async_copy(src, held, in_sem.at[number]))
        outs.append(pltpu.make_async_copy(held, dst, out_sem.at[number]))
        ins[-1].start()
    for came, goes in zip(ins, outs):
        came.wait()
        goes.start()
    for goes in outs:
        goes.wait()

def on_device(
    velocity_cotangent,
    vertical_inverse,
    sliding_speed,
    friction_coef,
    thawed_bed,
    basal_melt,
    storage_coef,
    owner_tile,
    channel_open,
    group_mix,
    control_map,
):
    shaped = [x.reshape(ROWS, LANES) for x in (sliding_speed, friction_coef, thawed_bed, basal_melt, storage_coef, owner_tile)]
    f32 = jnp.float32
    anywhere = pl.BlockSpec(memory_space=pltpu.HBM)
    vmem = pl.BlockSpec(memory_space=pltpu.VMEM)
    columns = pltpu.VMEM((ROWS, LANES), f32)
    padded = pltpu.VMEM((ROWS + 24, LANES), f32)
    numbers = pltpu.VMEM((ROWS, LANES), jnp.int32)
    messages = pltpu.VMEM(((TILES + 1) * MSG, LANES), f32)
    received = pltpu.VMEM(((TALL + 1) * MSG, LANES), f32)
    field = pltpu.VMEM((TALL, WIDE), f32)
    dma = pltpu.SemaphoreType.DMA
    results = pl.pallas_call(
        kernel,
        out_shape=(
            jax.ShapeDtypeStruct((LAYERS, COLUMNS), f32),
            jax.ShapeDtypeStruct((TILES, RUN * LANES), f32),
            jax.ShapeDtypeStruct((ROWS, LANES), f32),
            jax.ShapeDtypeStruct((1, CONTROLS), f32),
        ),
        in_specs=[pl.BlockSpec(memory_space=pltpu.SMEM), vmem] + [anywhere] * 9,
        out_specs=(anywhere, anywhere, anywhere, vmem),
        scratch_shapes=[
            pltpu.VMEM((LAYERS, COLUMNS), f32), pltpu.VMEM((LAYERS, COLUMNS), f32),
            pltpu.VMEM((CONTROLS, COLUMNS), jnp.bfloat16),
            columns, columns, numbers, padded, padded, numbers,
            pltpu.VMEM((TILES, RUN * LANES), jnp.int32),
            padded, columns,
            messages, messages, received, received, pltpu.VMEM(((2 * EDGE + 1) * MSG, LANES), f32),
            field, pltpu.VMEM((TILES, LANES), f32), pltpu.VMEM((TILES, LANES), f32),
            field, pltpu.VMEM((TILES, WIDE), f32), pltpu.VMEM((TILES, RUN * LANES), f32), messages,
        ]
        + [pltpu.VMEM((nodes, pad + tall, LANES), f32) for nodes, pad, tall in LEVELS]
        + [
            columns, pltpu.VMEM((CHIPS, ROWS, LANES), f32), columns, columns, columns,
            pltpu.SMEM((TILES + 1,), jnp.int32), dma((8,)), dma((PARTS,)), dma((3,)), dma((11,)), dma((11,)),
            dma((PARTS, CHIPS - 1)), dma((PARTS, CHIPS - 1)), dma((PARTS,)), dma((PARTS,)), dma((3,)),
        ],
        compiler_params=pltpu.CompilerParams(
            collective_id=0, has_side_effects=True, vmem_limit_bytes=VMEM_BYTES
        ),
    )(group_mix, vertical_inverse, velocity_cotangent, *shaped, channel_open, control_map)
    adjoint, pressure, sensitivity, gradient = pl.pallas_call(
        hand_on_kernel,
        out_shape=tuple(jax.ShapeDtypeStruct(x.shape, x.dtype) for x in results),
        in_specs=[anywhere] * 4,
        out_specs=(anywhere,) * 4,
        scratch_shapes=[pltpu.VMEM(x.shape, x.dtype) for x in results] + [dma((3 + PIECES,)), dma((3 + PIECES,))],
        compiler_params=pltpu.CompilerParams(vmem_limit_bytes=VMEM_BYTES),
    )(*results)
    return adjoint, pressure, sensitivity.reshape(COLUMNS), gradient.reshape(CONTROLS)


def solution(mesh):
    in_specs = (
        P(None, ("col", "grp")),
        P(),
        P(("col", "grp")),
        P(("col", "grp")),
        P(("col", "grp")),
        P(("col", "grp")),
        P(("col", "grp")),
        P(("col", "grp"), None),
        P("grp", "col"),
        P(),
        P(("col", "grp"), None),
    )
    out_specs = (P(None, ("col", "grp")), P("grp", "col"), P(("col", "grp")), P(("col", "grp")))
    return jax.shard_map(
        on_device, mesh=mesh, in_specs=in_specs, out_specs=out_specs, check_vma=False
    )
```

```python
import functools

import jax
import jax.numpy as jnp
from jax import lax
from jax.experimental import pallas as pl
from jax.experimental.pallas import tpu as pltpu
from jax.sharding import PartitionSpec as P

HSWEEPS = 4
diffusion_rate = 0.12
melt_rate = 0.3

TILES = 32
GROUP = 8
CHIPS = 4
RING_Y, RING_Z = 4, 8
COLUMNS = 32768
LAYERS = 20
LAYER_ROWS = 24
LANES = 128
ROWS = COLUMNS // LANES
RUN = 10
MSG = 16
MSG2 = 15
EDGE = 8
WIDE = RUN * LANES + LANES
TALL = TILES + 2 * EDGE
CONTROLS = 64
PIECES = 4
PARTS = 4
PART = ROWS // PARTS
PART_ORDER = [q + half for q in range(PARTS // 2) for half in (0, PARTS // 2)]
MESH = pl.DeviceIdType.MESH
VMEM_BYTES = 64 * 1024 * 1024

LEVELS = ((32, 16, 24), (16, 24, 40), (8, 48, 80), (4, 88, 160), (2, 168, 256))


def rows_at(start, count):
    return pl.ds(pl.multiple_of(start, 8), count)


def kernel(
    mix_ref, inverse_ref, cot_hbm, slide_hbm, fric_hbm, thaw_hbm, melt_hbm, store_hbm, owner_hbm, open_hbm, map_hbm,
    adj_hbm, press_hbm, sens_hbm, grad_ref,
    cot, adj, cmap, slide, fric, thaw, melt, store, owner, chan, source, basal,
    send1, send2, recv1, recv2, edge2, cond, cond_low, cond_high, coef, pressure, press_out, back_send,
    lev0, lev1, lev2, lev3, lev4, sens, gathered, other_send, other_recv, mine,
    begins, load_sem, cot_sem, self_sem, send_sem, recv_sem, part_send, part_recv, pair_send, pair_recv, out_sem,
):
    a = lax.axis_index("col")
    g = lax.axis_index("grp")
    chip = g // 2
    core = lax.rem(g, 2)
    sibling = chip * 2 + (1 - core)
    up = lax.rem(g + GROUP - 1, GROUP)
    down = lax.rem(g + 1, GROUP)
    left = lax.rem(a + TILES - 1, TILES)
    right = lax.rem(a + 1, TILES)

    def load(src, dst, number):
        copy = pltpu.make_async_copy(src, dst, load_sem.at[number])
        copy.start()
        return copy

    owner_load = load(owner_hbm, owner, 0)
    melt_load = load(melt_hbm, melt.at[pl.ds(0, ROWS)], 1)
    store_load = load(store_hbm, store.at[pl.ds(0, ROWS)], 2)
    barrier = pltpu.get_barrier_semaphore()

    def greet(d, carry):
        pl.semaphore_signal(
            barrier, inc=1, device_id={"col": lax.rem(a + d, TILES)}, device_id_type=MESH
        )
        return carry

    lax.fori_loop(1, TILES, greet, 0)
    for other in (up, down):
        pl.semaphore_signal(barrier, inc=1, device_id={"grp": other}, device_id_type=MESH)
    for d in (1, CHIPS - 1):
        same_core = lax.rem(chip + d, CHIPS) * 2 + core
        pl.semaphore_signal(barrier, inc=1, device_id={"grp": same_core}, device_id_type=MESH)

    cot_loads = []
    piece = COLUMNS // PARTS
    for q in range(PARTS):
        copy = pltpu.make_async_copy(
            cot_hbm.at[:, pl.ds(q * piece, piece)], cot.at[:, pl.ds(q * piece, piece)], cot_sem.at[q]
        )
        copy.start()
        cot_loads.append(copy)
    chan_load = load(open_hbm, chan, 3)
    thaw_load = load(thaw_hbm, thaw, 4)
    slide_load = load(slide_hbm, slide, 5)
    fric_load = load(fric_hbm, fric, 6)
    map_load = load(map_hbm, cmap, 7)

    lane = lax.broadcasted_iota(jnp.int32, (1, LANES), 1)
    edge_rows = jnp.zeros((4 * MSG, LANES), jnp.float32)
    recv1[0 : 4 * MSG, :] = edge_rows
    recv1[(TALL - 4) * MSG : TALL * MSG, :] = edge_rows
    edge2[0 : 4 * MSG, :] = edge_rows
    edge2[(EDGE + 4) * MSG : 2 * EDGE * MSG, :] = edge_rows

    owner_load.wait()
    owners = owner[...]
    starts = [jnp.int32(0)]
    for t in range(1, TILES):
        below = jnp.where(owners < t, 1.0, 0.0).astype(jnp.float32)
        partial = jnp.sum(below.reshape(ROWS // 8, 8, LANES), axis=0)
        starts.append(jnp.clip(jnp.sum(partial).astype(jnp.int32), 0, COLUMNS))
    starts.append(jnp.int32(COLUMNS))
    for t in range(TILES + 1):
        begins[t] = starts[t]

    slot = lax.broadcasted_iota(jnp.int32, (MSG, LANES), 0) * LANES + lax.broadcasted_iota(
        jnp.int32, (MSG, LANES), 1
    )

    def window(ref, begin, end):
        first = lax.shift_right_logical(begin, 7)
        turn = lax.bitwise_and(begin, LANES - 1)
        back_turn = lax.bitwise_and(LANES - turn, LANES - 1)
        low = pltpu.roll(ref[pl.ds(first, MSG), :], back_turn, 1)
        high = pltpu.roll(ref[pl.ds(first + 1, MSG), :], back_turn, 1)
        both = jnp.where(lane < LANES - turn, low, high)
        return jnp.where(slot < end - begin, both, 0.0)

    def post(src, dst, number, where):
        copy = pltpu.make_async_remote_copy(
            src_ref=src, dst_ref=dst, send_sem=send_sem.at[number], recv_sem=recv_sem.at[number],
            device_id=where, device_id_type=MESH,
        )
        copy.start()
        return copy

    def keep_own(src, dst, self_number, rows):
        own = pltpu.make_async_copy(
            src.at[rows_at(a * MSG, rows)], dst.at[rows_at((EDGE + a) * MSG, rows)], self_sem.at[self_number]
        )
        own.start()
        return own

    def outward(far, order):
        return far + (1 - 2 * (order % 2)) * ((order + 1) // 2)

    def far_first(order):
        away_z = outward(RING_Z // 2, order // RING_Y)
        away_y = outward(RING_Y // 2, order % RING_Y)
        return lax.rem(a // RING_Z + away_y, RING_Y) * RING_Z + lax.rem(a + away_z, RING_Z)

    def to_all(src, dst, number, self_number, rows):
        def one(order, carry):
            target = far_first(order)
            post(src.at[rows_at(target * MSG, rows)], dst.at[rows_at((EDGE + a) * MSG, rows)], number, {"col": target})
            return carry

        lax.fori_loop(0, TILES - 1, one, 0)
        return keep_own(src, dst, self_number, rows)

    def all_done(buffer, rows, sem):
        pltpu.make_async_copy(buffer.at[pl.ds(0, rows)], buffer.at[pl.ds(0, rows)], sem).wait()

    store_load.wait()
    melt_load.wait()
    for group in range(TILES // 8):
        targets = [far_first(order) for order in range(group * 8, (group + 1) * 8)]
        for t in targets:
            at = pl.multiple_of(t * MSG, MSG)
            begin, end = begins[t], begins[t + 1]
            stored = window(store, begin, end)
            melted = window(melt, begin, end)
            send1[pl.ds(at, RUN), :] = stored[:RUN]
            send1[pl.ds(at + RUN, MSG - RUN), :] = melted[: MSG - RUN]
            send2[pl.ds(at, 2 * RUN - MSG), :] = melted[MSG - RUN : RUN]
        if group == 0:
            pl.semaphore_wait(barrier, TILES - 1 + 2 + 2)
        for t in targets[: TILES - 1 - group * 8]:
            post(send1.at[rows_at(t * MSG, MSG)], recv1.at[rows_at((EDGE + a) * MSG, MSG)], 2, {"col": t})
    own1 = keep_own(send1, recv1, 0, MSG)
    chan_load.wait()
    cond[EDGE : EDGE + TILES, : RUN * LANES] = jnp.where(chan[...] == 1, diffusion_rate, 0.25 * diffusion_rate)
    chan_low = post(cond.at[EDGE : EDGE + TILES, (RUN - 1) * LANES : RUN * LANES], cond_low, 0, {"col": right})
    chan_high = post(cond.at[EDGE : EDGE + TILES, 0:LANES], cond_high, 1, {"col": left})

    weight = jnp.broadcast_to(inverse_ref[:, LAYERS - 1 : LAYERS], (LAYERS, LANES))
    sublane = lax.broadcasted_iota(jnp.int32, (8, LANES), 0)
    thaw_load.wait()
    slide_load.wait()
    fric_load.wait()
    for q in range(PARTS):
        cot_loads[q].wait()

        def last_layer(j, carry):
            block = jnp.zeros((8, LANES), jnp.float32)
            for k in range(8):
                layers = cot[:, pl.ds(pl.multiple_of(j * 1024 + k * LANES, LANES), LANES)]
                total = jnp.sum(layers * weight, axis=0, keepdims=True)
                block = jnp.where(sublane == k, total, block)
            at = rows_at(j * 8, 8)
            base = thaw[at, :].astype(jnp.float32) * slide[at, :] * block
            basal[at, :] = base
            source[at, :] = fric[at, :] * base
            return carry

        lax.fori_loop(q * 8, (q + 1) * 8, last_layer, 0)

    for t in range(TILES):
        send2[MSG * t + 2 * RUN - MSG : MSG * t + 3 * RUN - MSG, :] = window(source, starts[t], starts[t + 1])[:RUN]

    tile = lax.broadcasted_iota(jnp.int32, (TILES, LANES), 0)
    lanes = lax.broadcasted_iota(jnp.int32, (TILES, LANES), 1)

    def beside(first, last):
        ahead = jnp.where(tile == TILES - 1, 0.0, pltpu.roll(first, TILES - 1, 0))
        behind = jnp.where(tile == 0, 0.0, pltpu.roll(last, 1, 0))
        return jnp.where(lanes < 4, ahead, jnp.where(lanes >= LANES - 4, behind, 0.0))

    def every(ref, row):
        return ref[pl.ds(row, TILES, stride=MSG), :]

    source_sides = beside(every(send2, 4), every(send2, 13))
    melt_sides = beside(every(send1, 10), every(send2, 3))
    store_sides = beside(every(send1, 0), every(send1, 9))

    def moved_in(sides, by):
        return jnp.where(lanes < 64, pltpu.roll(sides, by, 1), pltpu.roll(sides, LANES - by, 1))

    def outer(count):
        return jnp.logical_or(lanes < count, lanes >= LANES - count)

    send2[pl.ds(14, TILES, stride=MSG), :] = jnp.where(
        outer(4), source_sides, jnp.where(outer(8), moved_in(melt_sides, 4), moved_in(store_sides, 8))
    )
    own2 = to_all(send2, recv2, 3, 1, MSG2)

    tall = 8 * LAYER_ROWS
    half = jnp.bfloat16
    dot = functools.partial(jnp.dot, preferred_element_type=jnp.float32)
    layer = lax.rem(lax.broadcasted_iota(jnp.int32, (tall, LAYERS), 0), LAYER_ROWS)
    spread = (layer == lax.broadcasted_iota(jnp.int32, (tall, LAYERS), 1)).astype(jnp.float32).astype(half)
    block = lax.broadcasted_iota(jnp.int32, (tall, tall), 0) // LAYER_ROWS
    own_block = block == lax.broadcasted_iota(jnp.int32, (tall, tall), 1) // LAYER_ROWS

    def diagonal(part):
        rows = dot(spread, part).astype(half)
        full = lax.dot_general(rows, spread, (((1,), (1,)), ((), ())), preferred_element_type=jnp.float32)
        return jnp.where(own_block, full, 0.0).astype(half)

    matrix = inverse_ref[...].T
    matrix_high = matrix.astype(half)
    high = diagonal(matrix_high)
    low = diagonal((matrix - matrix_high.astype(jnp.float32)).astype(half))
    pad = jnp.zeros((LAYER_ROWS - LAYERS, 2 * LANES), jnp.float32)
    step = 16 * LANES

    def product_of(n, carry):
        def columns_of(k):
            return pl.ds(pl.multiple_of(n * step + 2 * k * LANES, 2 * LANES), 2 * LANES)

        tiles = []
        for k in range(8):
            tiles += [cot[:, columns_of(k)], pad]
        values = jnp.concatenate(tiles, axis=0)
        values_high = values.astype(half)
        values_low = (values - values_high.astype(jnp.float32)).astype(half)
        result = dot(high, values_high) + (dot(high, values_low) + dot(low, values_high))
        for k in range(8):
            adj[:, columns_of(k)] = result[k * LAYER_ROWS : k * LAYER_ROWS + LAYERS]
        return carry

    lax.fori_loop(0, COLUMNS // step, product_of, 0)
    adj_copy = pltpu.make_async_copy(adj, adj_hbm, out_sem.at[2])
    adj_copy.start()

    chan_low.wait_recv()
    chan_high.wait_recv()
    low_side = jnp.where(jnp.logical_and(lanes >= LANES - 4, a > 0), cond_low[...], 0.0)
    cond[EDGE : EDGE + TILES, RUN * LANES :] = jnp.where(
        jnp.logical_and(lanes < 4, a < TILES - 1), cond_high[...], low_side
    )
    chan_up = post(cond.at[pl.ds(EDGE, EDGE)], cond.at[pl.ds(EDGE + TILES, EDGE)], 4, {"grp": up})
    chan_down = post(cond.at[pl.ds(TILES, EDGE)], cond.at[pl.ds(0, EDGE)], 5, {"grp": down})

    def rows_beside(buffer, into, below, number):
        first = post(buffer.at[pl.ds(EDGE * MSG, 4 * MSG)], into.at[pl.ds(below, 4 * MSG)], number, {"grp": up})
        second = post(
            buffer.at[pl.ds((TILES + 4) * MSG, 4 * MSG)], into.at[pl.ds(4 * MSG, 4 * MSG)], number + 1, {"grp": down}
        )
        return first, second

    others = (TILES - 1) * MSG
    own1.wait()
    all_done(recv1, others, recv_sem.at[2])
    rows1 = rows_beside(recv1, recv1, (EDGE + TILES) * MSG, 6)
    chan_up.wait_recv()
    chan_down.wait_recv()
    for copy in rows1:
        copy.wait_recv()

    row = lax.broadcasted_iota(jnp.int32, (TALL, LANES), 0)
    inside = jnp.logical_and(
        jnp.logical_or(row >= EDGE, g > 0), jnp.logical_or(row < EDGE + TILES, g < GROUP - 1)
    )

    def mesh_rows(ref, k):
        return ref[pl.ds(k, TALL, stride=MSG), :]

    for k in range(RUN):
        at = slice(k * LANES, (k + 1) * LANES)
        coef[:, at] = jnp.where(inside, cond[:, at] / (1.0 + mesh_rows(recv1, k)), 0.0)

    own2.wait()
    all_done(recv2, (TILES - 1) * MSG2, recv_sem.at[3])
    rows2 = rows_beside(recv2, edge2, EDGE * MSG, 8)

    last = slice(RUN * LANES, WIDE)
    lane_tall = lax.broadcasted_iota(jnp.int32, (TILES, LANES), 1)
    used = jnp.logical_or(lane_tall < 4, lane_tall >= LANES - 4)

    def sweeps(got1, got2, inside, rate_of):
        side = got2(14)

        def moved_out(by):
            back = jnp.where(lane_tall < 64, pltpu.roll(side, LANES - by, 1), pltpu.roll(side, by, 1))
            return jnp.where(used, back, 0.0)

        store_side = moved_out(8)
        melts = [got1(RUN + k) for k in range(MSG - RUN)]
        melts += [got2(k) for k in range(2 * RUN - MSG)] + [moved_out(4)]
        keep = jnp.concatenate([1.0 - melt_rate * part for part in melts], axis=1)
        rate_side = jnp.where(inside, rate_of(cond, last) / (1.0 + store_side), 0.0)
        rate = jnp.concatenate([rate_of(coef, slice(0, RUN * LANES)), rate_side], axis=1)
        pressure[...] = jnp.concatenate(
            [jnp.where(inside, got2(2 * RUN - MSG + k), 0.0) for k in range(RUN)]
            + [jnp.where(jnp.logical_and(inside, used), side, 0.0)],
            axis=1,
        )
        for sweep in range(HSWEEPS):
            field = pressure[...]
            sides = (
                pltpu.roll(field, 1, 1)
                + pltpu.roll(field, WIDE - 1, 1)
                + pltpu.roll(field, 1, 0)
                + pltpu.roll(field, TILES - 1, 0)
            )
            pressure[...] = keep * field + rate * (sides - 4.0 * field)

    def own_rows(ref):
        return lambda k: ref[pl.ds(EDGE * MSG + k, TILES, stride=MSG), :]

    pad0 = LEVELS[0][1]

    def give_back(target):
        post(back_send.at[rows_at(target * MSG, RUN)], lev0.at[a, pl.ds(pad0, RUN)], 10, {"col": target})

    def middle_back(order, carry):
        target = far_first(order)

        @pl.when(jnp.logical_and(target >= 4, target < TILES - 4))
        def _():
            give_back(target)

        return carry

    def edge_back(order, carry):
        number = lax.rem(a + order, 8)
        target = number + (number // 4) * (TILES - 8)

        @pl.when(target != a)
        def _():
            give_back(target)

        return carry

    sweeps(own_rows(recv1), own_rows(recv2), True, lambda ref, at: ref[EDGE : EDGE + TILES, at])
    for k in range(RUN):
        at = slice(k * LANES, (k + 1) * LANES)
        for i in range(TILES // 8):
            back_send[pl.ds(8 * i * MSG + k, 8, stride=MSG), :] = pressure[8 * i : 8 * i + 8, at]
    press_out[...] = pressure[:, : RUN * LANES]
    lax.fori_loop(0, TILES - 1, middle_back, 0)

    for copy in rows2:
        copy.wait_recv()

    def band(ref, k):
        return [ref[pl.ds(row * MSG + k, EDGE, stride=MSG), :] for row in (EDGE, TILES)]

    def edge_rows1(k):
        outer = [recv1[pl.ds(row * MSG + k, EDGE, stride=MSG), :] for row in (0, EDGE + TILES)]
        inner = band(recv1, k)
        return jnp.concatenate([outer[0], inner[0], inner[1], outer[1]], axis=0)

    def edge_rows2(k):
        outer = [edge2[pl.ds(row * MSG + k, EDGE, stride=MSG), :] for row in (0, EDGE)]
        inner = band(recv2, k)
        return jnp.concatenate([outer[0], inner[0], inner[1], outer[1]], axis=0)

    band_row = lax.broadcasted_iota(jnp.int32, (TILES, LANES), 0)
    band_inside = jnp.logical_and(
        jnp.logical_or(band_row >= EDGE, g > 0), jnp.logical_or(band_row < TILES - EDGE, g < GROUP - 1)
    )
    sweeps(
        edge_rows1, edge_rows2, band_inside,
        lambda ref, at: jnp.concatenate([ref[0 : 2 * EDGE, at], ref[TILES:TALL, at]], axis=0),
    )
    for k in range(RUN):
        at = slice(k * LANES, (k + 1) * LANES)
        back_send[pl.ds(k, 4, stride=MSG), :] = pressure[EDGE : EDGE + 4, at]
        back_send[pl.ds((TILES - 4) * MSG + k, 4, stride=MSG), :] = pressure[2 * EDGE + 4 : 3 * EDGE, at]
    lax.fori_loop(0, 8, edge_back, 0)
    press_out[0:4, :] = pressure[EDGE : EDGE + 4, : RUN * LANES]
    press_out[TILES - 4 : TILES, :] = pressure[2 * EDGE + 4 : 3 * EDGE, : RUN * LANES]
    press_copy = pltpu.make_async_copy(press_out, press_hbm, out_sem.at[0])
    press_copy.start()
    own_back = pltpu.make_async_copy(
        back_send.at[rows_at(a * MSG, RUN)], lev0.at[a, pl.ds(pad0, RUN)], self_sem.at[2]
    )
    own_back.start()
    own_back.wait()
    all_done(back_send, (TILES - 1) * RUN, recv_sem.at[10])

    def pass_on(q, slot, src, ahead):
        copy = pltpu.make_async_remote_copy(
            src_ref=src.at[pl.ds(q * PART, PART)],
            dst_ref=gathered.at[slot, pl.ds(q * PART, PART)],
            send_sem=part_send.at[q, slot - 1],
            recv_sem=part_recv.at[q, slot - 1],
            device_id={"grp": lax.rem(chip + ahead, CHIPS) * 2 + core},
            device_id_type=MESH,
        )
        copy.start()
        return copy

    parts = {}

    def merge(ref, node, pad, length, begin, rows):
        first = lax.shift_right_logical(length, 7)
        turn = lax.bitwise_and(length, LANES - 1)
        index = lax.broadcasted_iota(jnp.int32, (rows, LANES), 0) * LANES + lax.broadcasted_iota(
            jnp.int32, (rows, LANES), 1
        )
        head = ref[2 * node, pl.ds(pad + begin, rows), :]
        here = pltpu.roll(ref[2 * node + 1, pl.ds(pad + begin - first, rows), :], turn, 1)
        before = pltpu.roll(ref[2 * node + 1, pl.ds(pad + begin - 1 - first, rows), :], turn, 1)
        return jnp.where(index < length - begin * LANES, head, jnp.where(lane >= turn, here, before))

    levels = (lev0, lev1, lev2, lev3, lev4)
    for level, (nodes, pad, tall) in enumerate(LEVELS):
        ref = levels[level]
        for node in range(nodes // 2):
            begin = starts[(2 * node) << level]
            length = jnp.clip(starts[(2 * node + 1) << level] - begin, 0, (RUN << level) * LANES)
            for part, rows in ((0, tall),) if level < len(LEVELS) - 1 else tuple((q, PART) for q in PART_ORDER):
                merged = merge(ref, node, pad, length, part * rows, rows)
                if level < len(LEVELS) - 1:
                    levels[level + 1][node, pl.ds(LEVELS[level + 1][1], tall), :] = merged
                else:
                    at = pl.ds(part * PART, PART)
                    sens[at, :] = thaw[at, :].astype(jnp.float32) * fric[at, :] * (basal[at, :] + merged)
                    if part < PARTS // 2:
                        parts[part, 1] = pass_on(part, 1, sens, 1)
                    else:
                        parts[part, 3] = pass_on(part, 3, sens, CHIPS - 1)

    sens_copy = pltpu.make_async_copy(sens, sens_hbm, out_sem.at[1])
    sens_copy.start()

    for q in range(PARTS // 2):
        other = q + PARTS // 2
        parts[other, 1] = pass_on(other, 1, sens, 1)
        parts[q, 3] = pass_on(q, 3, sens, CHIPS - 1)
    in_order = []
    for q in range(PARTS // 2):
        other = q + PARTS // 2
        parts[q, 1].wait_recv()
        parts[q, 2] = pass_on(q, 2, gathered.at[1], 1)
        parts[other, 3].wait_recv()
        parts[other, 2] = pass_on(other, 2, gathered.at[3], CHIPS - 1)
        in_order += [q, other]

    def factor(who, d):
        return mix_ref[who, lax.rem(chip + CHIPS - d, CHIPS) * 2 + core]

    to_self = [factor(g, d) for d in range(CHIPS)]
    to_other = [factor(sibling, d) for d in range(CHIPS)]
    pairs = {}
    for q in in_order:
        at = pl.ds(q * PART, PART)
        parts[q, 3 if q < PARTS // 2 else 1].wait_recv()
        parts[q, 2].wait_recv()
        pieces = [sens[at, :]] + [gathered[d, at, :] for d in range(1, CHIPS)]
        other_send[at, :] = sum(to_other[d] * pieces[d] for d in range(CHIPS))
        copy = pltpu.make_async_remote_copy(
            src_ref=other_send.at[at], dst_ref=other_recv.at[at], send_sem=pair_send.at[q], recv_sem=pair_recv.at[q],
            device_id={"grp": sibling}, device_id_type=MESH,
        )
        copy.start()
        pairs[q] = copy
        mine[at, :] = sum(to_self[d] * pieces[d] for d in range(CHIPS))

    map_load.wait()
    total = jnp.zeros((CONTROLS, LANES), jnp.float32)
    for q in in_order:
        pairs[q].wait_recv()

        def product(j, total):
            at = rows_at(j * 8, 8)
            mixed = (mine[at, :] + other_recv[at, :]).astype(jnp.bfloat16).astype(jnp.float32)
            for s in range(8):
                block = cmap[:, pl.ds(pl.multiple_of(j * 1024 + s * LANES, LANES), LANES)]
                total = total + block.astype(jnp.float32) * mixed[s : s + 1, :]
            return total

        total = lax.fori_loop(q * PART // 8, (q + 1) * PART // 8, product, total)
    grad_ref[...] = jnp.sum(total.T, axis=0, keepdims=True)

    chan_low.wait_send()
    chan_high.wait_send()
    chan_up.wait_send()
    chan_down.wait_send()
    for copy in rows1 + rows2:
        copy.wait_send()
    all_done(send1, others, send_sem.at[2])
    all_done(send2, (TILES - 1) * MSG2, send_sem.at[3])
    all_done(back_send, (TILES - 1) * RUN, send_sem.at[10])
    for copy in list(parts.values()) + list(pairs.values()):
        copy.wait_send()
    press_copy.wait()
    sens_copy.wait()
    adj_copy.wait()


def hand_on_kernel(
    adj_in, press_in, sens_in, grad_in, adj_out, press_out, sens_out, grad_out, adj, press, sens, grad, in_sem, out_sem
):
    width = COLUMNS // PIECES
    moves = [(press_in, press, press_out), (sens_in, sens, sens_out), (grad_in, grad, grad_out)]
    for q in range(PIECES):
        at = pl.ds(q * width, width)
        moves.append((adj_in.at[:, at], adj.at[:, at], adj_out.at[:, at]))
    ins, outs = [], []
    for number, (src, held, dst) in enumerate(moves):
        ins.append(pltpu.make_async_copy(src, held, in_sem.at[number]))
        outs.append(pltpu.make_async_copy(held, dst, out_sem.at[number]))
        ins[-1].start()
    for came, goes in zip(ins, outs):
        came.wait()
        goes.start()
    for goes in outs:
        goes.wait()

def on_device(
    velocity_cotangent,
    vertical_inverse,
    sliding_speed,
    friction_coef,
    thawed_bed,
    basal_melt,
    storage_coef,
    owner_tile,
    channel_open,
    group_mix,
    control_map,
):
    shaped = [x.reshape(ROWS, LANES) for x in (sliding_speed, friction_coef, thawed_bed, basal_melt, storage_coef, owner_tile)]
    f32 = jnp.float32
    anywhere = pl.BlockSpec(memory_space=pltpu.HBM)
    vmem = pl.BlockSpec(memory_space=pltpu.VMEM)
    columns = pltpu.VMEM((ROWS, LANES), f32)
    padded = pltpu.VMEM((ROWS + 24, LANES), f32)
    numbers = pltpu.VMEM((ROWS, LANES), jnp.int32)
    messages = pltpu.VMEM(((TILES + 1) * MSG, LANES), f32)
    received = pltpu.VMEM(((TALL + 1) * MSG, LANES), f32)
    field = pltpu.VMEM((TALL, WIDE), f32)
    dma = pltpu.SemaphoreType.DMA
    results = pl.pallas_call(
        kernel,
        out_shape=(
            jax.ShapeDtypeStruct((LAYERS, COLUMNS), f32),
            jax.ShapeDtypeStruct((TILES, RUN * LANES), f32),
            jax.ShapeDtypeStruct((ROWS, LANES), f32),
            jax.ShapeDtypeStruct((1, CONTROLS), f32),
        ),
        in_specs=[pl.BlockSpec(memory_space=pltpu.SMEM), vmem] + [anywhere] * 9,
        out_specs=(anywhere, anywhere, anywhere, vmem),
        scratch_shapes=[
            pltpu.VMEM((LAYERS, COLUMNS), f32), pltpu.VMEM((LAYERS, COLUMNS), f32),
            pltpu.VMEM((CONTROLS, COLUMNS), jnp.bfloat16),
            columns, columns, numbers, padded, padded, numbers,
            pltpu.VMEM((TILES, RUN * LANES), jnp.int32),
            padded, columns,
            messages, messages, received, received, pltpu.VMEM(((2 * EDGE + 1) * MSG, LANES), f32),
            field, pltpu.VMEM((TILES, LANES), f32), pltpu.VMEM((TILES, LANES), f32),
            field, pltpu.VMEM((TILES, WIDE), f32), pltpu.VMEM((TILES, RUN * LANES), f32), messages,
        ]
        + [pltpu.VMEM((nodes, pad + tall, LANES), f32) for nodes, pad, tall in LEVELS]
        + [
            columns, pltpu.VMEM((CHIPS, ROWS, LANES), f32), columns, columns, columns,
            pltpu.SMEM((TILES + 1,), jnp.int32), dma((8,)), dma((PARTS,)), dma((3,)), dma((11,)), dma((11,)),
            dma((PARTS, CHIPS - 1)), dma((PARTS, CHIPS - 1)), dma((PARTS,)), dma((PARTS,)), dma((3,)),
        ],
        compiler_params=pltpu.CompilerParams(
            collective_id=0, has_side_effects=True, vmem_limit_bytes=VMEM_BYTES
        ),
    )(group_mix, vertical_inverse, velocity_cotangent, *shaped, channel_open, control_map)
    adjoint, pressure, sensitivity, gradient = pl.pallas_call(
        hand_on_kernel,
        out_shape=tuple(jax.ShapeDtypeStruct(x.shape, x.dtype) for x in results),
        in_specs=[anywhere] * 4,
        out_specs=(anywhere,) * 4,
        scratch_shapes=[pltpu.VMEM(x.shape, x.dtype) for x in results] + [dma((3 + PIECES,)), dma((3 + PIECES,))],
        compiler_params=pltpu.CompilerParams(vmem_limit_bytes=VMEM_BYTES),
    )(*results)
    return adjoint, pressure, sensitivity.reshape(COLUMNS), gradient.reshape(CONTROLS)


def solution(mesh):
    in_specs = (
        P(None, ("col", "grp")),
        P(),
        P(("col", "grp")),
        P(("col", "grp")),
        P(("col", "grp")),
        P(("col", "grp")),
        P(("col", "grp")),
        P(("col", "grp"), None),
        P("grp", "col"),
        P(),
        P(("col", "grp"), None),
    )
    out_specs = (P(None, ("col", "grp")), P("grp", "col"), P(("col", "grp")), P(("col", "grp")))
    return jax.shard_map(
        on_device, mesh=mesh, in_specs=in_specs, out_specs=out_specs, check_vma=False
    )
```
